256 devices in a mesh: step: 8 (over z), seq: 32 (over y, x, core).
Axes of the slice: x: 4, y: 4, z: 8, core: 2. Of those that a mesh axis runs over, the one named last changes fastest.
Arguments:
- trajectory: float32 [8, 2, 1024, 64], P('step', None, 'seq'), may hold values from -3 to 3
- noise: float32 [8, 2, 1024, 64], P('step', None, 'seq'), may hold values from -1.5 to 1.5
- step_sizes: float32 [8], P('step'), may hold values from 0.1 to 0.3
- modulation: float32 [8, 7, 3072], P('step'), may hold values from -3 to 3
- text_states: bfloat16 [2, 512, 3072], P(None, 'seq'), may hold values from -3.5 to 3.5
- w_latent: bfloat16 [64, 3072], replicated, may hold values from -0.75 to 0.75
- w_image_qkv: bfloat16 [3072, 3, 16, 128], P('seq'), may hold values from -0.054487432 to 0.054487432
- w_text_kv: bfloat16 [3072, 2, 16, 128], P('seq'), may hold values from -0.109375 to 0.109375
- w_out_t: bfloat16 [3072, 16, 128], P('seq'), may hold values from -0.125 to 0.125
- qk_gains: float32 [3, 128], replicated, may hold values from 0.5 to 1.5
- w_final: bfloat16 [3072, 64], replicated, may hold values from -0.109375 to 0.109375
Outputs:
- trajectory_out: float32 [8, 2, 1024, 64], P('step', None, 'seq')
The draws below stay inside these ranges and needn't reach their ends.
All inputs are finite; a program needn't handle non-finite values.
Results may differ from the reference program's by a relative error of at most 0.0025.
Values may be sent and summed in bfloat16 or wider, within the bound.
No kernel may reach another device: no remote copies, remote signals or barrier semaphores. Data moves between devices by JAX's collectives and lax.ppermute only.
A program may use at most 128 MiB of HBM per device.

```python
import math
import jax
import jax.numpy as jnp
from jax import lax

D = 3072
HD = 128
C = 64
HEADS = 16
L_IMG = 1024
L_TXT = 512
IMAGES = 2
ITERS = 2
STEPS = 8


def draw_trajectory(key, part):
    key = jax.random.fold_in(key, 7)
    order_key, centre_key, spread_key = jax.random.split(key, 3)
    orders = jax.vmap(lambda subkey: jax.random.permutation(subkey, L_IMG))(jax.random.split(order_key, IMAGES))
    labels = orders // 16
    cluster_count = L_IMG // 16
    centres = jax.random.normal(centre_key, (IMAGES, cluster_count, C), jnp.float32)
    roughness = 0.3 * jax.random.normal(spread_key, (STEPS, IMAGES, L_IMG, C), jnp.float32)
    picked = jax.vmap(lambda centre_table, member_rows: centre_table[member_rows])(centres, labels)
    return jnp.clip(picked[None] + roughness, -3.0, 3.0)


def draw_text_states(key, part):
    key = jax.random.fold_in(key, 13)
    order_key, centre_key, spread_key = jax.random.split(key, 3)
    orders = jax.vmap(lambda subkey: jax.random.permutation(subkey, L_TXT))(jax.random.split(order_key, IMAGES))
    labels = orders // 16
    cluster_count = L_TXT // 16
    centres = jax.random.normal(centre_key, (IMAGES, cluster_count, D), jnp.float32)
    roughness = 0.3 * jax.random.normal(spread_key, (IMAGES, L_TXT, D), jnp.float32)
    picked = jax.vmap(lambda centre_table, member_rows: centre_table[member_rows])(centres, labels)
    return jnp.clip(picked + roughness, -3.5, 3.5).astype(jnp.bfloat16)


def draw_w_image_qkv(key, part):
    key = jax.random.fold_in(key, 19)
    base_key, other_key, value_key = jax.random.split(key, 3)
    block_shape = (D, HEADS, HD)
    query_part = jax.random.normal(base_key, block_shape, jnp.float32)
    other_part = jax.random.normal(other_key, block_shape, jnp.float32)
    value_part = jax.random.normal(value_key, block_shape, jnp.float32)
    key_part = 0.65 * query_part + 0.76 * other_part
    stacked = jnp.stack([query_part, key_part, value_part], axis=1)
    stacked = jnp.clip(stacked, -3.0, 3.0) * (1.0 / math.sqrt(D))
    return stacked.astype(jnp.bfloat16)


def level_of(own_key, dims, cuts, smallest, top_value):
    def one(position, shards_of):
        steps = jax.random.uniform(jax.random.fold_in(jax.random.fold_in(own_key, 6), position), (shards_of,), jnp.float32, smallest / len(cuts), top_value / len(cuts))
        return jnp.repeat(jnp.exp(steps), dims[position] // shards_of).reshape((-1,) + (1,) * (len(dims) - position - 1))

    factor_of = one(*cuts[0])
    for cut in cuts[1:]:
        factor_of = factor_of * one(*cut)
    return factor_of


def normal_values(own_key, extent, scale, reach, cuts=(), kind=jnp.bfloat16):
    entries = jax.random.normal(own_key, extent, jnp.float32) * scale
    if len(cuts) > 0:
        entries = level_of(own_key, extent, cuts, -0.22, 0.18) * entries
    return jnp.clip(entries, min=-reach, max=reach).astype(kind)


def setup_inputs(seed: int = 0) -> dict:
    splits = jax.random.split(jax.random.key(seed), 12)
    trajectory = draw_trajectory(jax.random.fold_in(splits[11], 71), 0)
    noise = normal_values(splits[1], (STEPS, IMAGES, L_IMG, C), 0.1, 1.5, ((0, 8), (2, 32)), jnp.float32)
    step_sizes = jnp.clip(jnp.exp(math.log(0.3) - 1.0986123 * jax.random.uniform(splits[2], (STEPS,), jnp.float32) ** level_of(splits[2], (STEPS,), ((0, 8),), -0.2, 0.2)), 0.1, 0.3)
    modulation = normal_values(splits[3], (STEPS, 7, D), 0.5, 3.0, ((0, 8),), jnp.float32)
    text_states = draw_text_states(jax.random.fold_in(splits[11], 71), 0)
    w_latent = normal_values(splits[5], (C, D), C ** -0.5, 0.75)
    w_image_qkv = draw_w_image_qkv(jax.random.fold_in(splits[11], 71), 0)
    w_text_kv = normal_values(splits[7], (D, 2, HEADS, HD), D ** -0.5, 0.109375, ((0, 32),))
    w_out_t = normal_values(splits[8], (D, HEADS, HD), (HEADS * HD) ** -0.5, 0.125, ((0, 32),))
    qk_gains = jnp.clip(1.0 + 0.1 * jax.random.normal(splits[9], (3, HD), jnp.float32), 0.5, 1.5)
    w_final = normal_values(splits[10], (D, C), D ** -0.5, 0.109375)
    return dict(trajectory=trajectory, noise=noise, step_sizes=step_sizes, modulation=modulation, text_states=text_states, w_latent=w_latent, w_image_qkv=w_image_qkv, w_text_kv=w_text_kv, w_out_t=w_out_t, qk_gains=qk_gains, w_final=w_final)


def layer_norm(values):
    centre = values - lax.optimization_barrier(jnp.mean(values, axis=-1, keepdims=True))
    spread = lax.optimization_barrier(jnp.mean(centre * centre, axis=-1, keepdims=True))
    return centre * lax.rsqrt(spread + 1e-06)

def rms_scale(values, gains):
    return values * lax.rsqrt(lax.optimization_barrier(jnp.mean(values * values, axis=-1, keepdims=True)) + 1e-06) * gains

def denoise(latent, text_norm, shifts, w_latent, w_image_qkv, w_text_kv, w_out_t, qk_gains, w_final):
    hidden = jnp.dot(latent, w_latent, preferred_element_type=jnp.float32)
    image_in = (layer_norm(hidden) * (1.0 + shifts[1]) + shifts[0]).astype(jnp.bfloat16)
    text_in = (text_norm.astype(jnp.float32) * (1.0 + shifts[4]) + shifts[3]).astype(jnp.bfloat16)
    factor = 1.0 / math.sqrt(HD)

    def one_head(head):
        image_w = lax.dynamic_index_in_dim(w_image_qkv, head, 2, keepdims=False)
        text_w = lax.dynamic_index_in_dim(w_text_kv, head, 2, keepdims=False)
        queries = rms_scale(jnp.dot(image_in, image_w[:, 0], preferred_element_type=jnp.float32), qk_gains[0]).astype(jnp.bfloat16)
        image_keys = rms_scale(jnp.dot(image_in, image_w[:, 1], preferred_element_type=jnp.float32), qk_gains[1]).astype(jnp.bfloat16)
        image_values = jnp.dot(image_in, image_w[:, 2], preferred_element_type=jnp.float32).astype(jnp.bfloat16)
        text_keys = rms_scale(jnp.dot(text_in, text_w[:, 0], preferred_element_type=jnp.float32), qk_gains[2]).astype(jnp.bfloat16)
        text_values = jnp.dot(text_in, text_w[:, 1], preferred_element_type=jnp.float32).astype(jnp.bfloat16)
        keys = jnp.concatenate([text_keys, image_keys], axis=0)
        values = jnp.concatenate([text_values, image_values], axis=0)
        scores = jnp.dot(queries, keys.T, preferred_element_type=jnp.float32) * factor
        powers = jnp.exp(scores)
        probs = (powers / lax.optimization_barrier(jnp.sum(powers, axis=-1, keepdims=True))).astype(jnp.bfloat16)
        return jnp.dot(probs, values, preferred_element_type=jnp.float32).astype(jnp.bfloat16)
    heads_out = lax.map(one_head, jnp.arange(HEADS, dtype=jnp.int32))
    mixed = jnp.einsum('hte,dhe->td', heads_out.astype(jnp.float32), w_out_t.astype(jnp.float32))
    combined = hidden + shifts[2] * mixed
    final_in = (layer_norm(combined) * (1.0 + shifts[6]) + shifts[5]).astype(jnp.bfloat16)
    return jnp.dot(final_in, w_final, preferred_element_type=jnp.float32)

def reference(trajectory, noise, step_sizes, modulation, text_states, w_latent, w_image_qkv, w_text_kv, w_out_t, qk_gains, w_final):
    text_norm = layer_norm(text_states.astype(jnp.float32)).astype(jnp.bfloat16)
    start = trajectory[0]
    current = trajectory
    totals = trajectory
    for iteration in range(ITERS):
        per_step = []
        for step in range(STEPS):
            drifts = []
            for image in range(IMAGES):
                drifts.append(denoise(current[step, image].astype(jnp.bfloat16), text_norm[image], modulation[step], w_latent, w_image_qkv, w_text_kv, w_out_t, qk_gains, w_final))
            per_step.append(step_sizes[step] * jnp.stack(drifts) + noise[step])
        increments = jnp.stack(per_step)
        increments = increments.at[0].add(start)
        totals = jnp.cumsum(increments, axis=0)
        current = jnp.concatenate([start[None], totals[:-1]], axis=0)
    return totals
```

```python
import math

import jax
import jax.numpy as jnp
from jax import lax
from jax.sharding import Mesh
from jax.sharding import PartitionSpec as P

ITERS = 2
CHIPS = ("y", "x")
SEQ = ("y", "x", "core")
F32, BF16 = jnp.float32, jnp.bfloat16


def layer_norm(values):
    centre = values - jnp.mean(values, axis=-1, keepdims=True)
    spread = jnp.mean(centre * centre, axis=-1, keepdims=True)
    return centre * lax.rsqrt(spread + 1e-06)


def rms_scale(values, gains):
    return values * lax.rsqrt(jnp.mean(values * values, axis=-1, keepdims=True) + 1e-06) * gains


def split_high(values):
    high = lax.reduce_precision(values, 8, 7)
    return high.astype(BF16), (values - high).astype(BF16)


def swap_cores(values):
    return lax.ppermute(values, "core", [(0, 1), (1, 0)])


def local(
    trajectory,
    noise,
    step_sizes,
    modulation,
    text_states,
    w_latent,
    w_image_qkv,
    w_text_kv,
    w_out_t,
    qk_gains,
    w_final,
):
    steps = lax.axis_size("step")
    chips = lax.axis_size(CHIPS)
    place, core, chip = lax.axis_index("step"), lax.axis_index("core"), lax.axis_index(CHIPS)
    seq = lax.axis_index(SEQ)
    images, rows, chans = trajectory.shape[1:]
    width = w_latent.shape[1]
    part, heads, hd = w_out_t.shape
    text_rows = text_states.shape[1] // steps
    shifts = modulation[0]
    factor = 1.0 / math.sqrt(hd)

    w_out = lax.all_gather(w_out_t.reshape(part, heads * hd), SEQ, tiled=True)

    mods = lax.all_to_all(
        jnp.broadcast_to(shifts[None, 3:5], (steps, 2, width)), "step", 0, 0, tiled=True
    )

    text_mine = lax.dynamic_slice_in_dim(text_states, place * text_rows, text_rows, 1)
    text_norm = layer_norm(text_mine.astype(F32)).astype(BF16)
    text_block = jnp.broadcast_to(
        text_norm.reshape(1, images, text_rows * width // hd, hd),
        (chips, images, text_rows * width // hd, hd),
    ).reshape(chips * images, -1, hd)
    weight_block = jnp.transpose(w_text_kv, (2, 1, 0, 3)).reshape(2 * heads, part, hd)
    latent = trajectory[0].astype(BF16)
    latent = jnp.concatenate([latent, latent], axis=-1)
    latent_block = jnp.broadcast_to(latent[None], (chips, images, rows, 2 * chans)).reshape(
        chips * images, rows, 2 * chans
    )
    packed = jnp.concatenate([weight_block, text_block, latent_block], axis=1)
    packed = lax.all_to_all(packed, SEQ, 0, 0, tiled=True)
    cut = packed.shape[1] - rows
    w_text_mine = packed[:, :part].reshape(width, hd)
    text_here = packed[:, part:cut].reshape(-1, width)
    latents = packed[:, cut:].reshape(-1, 2 * chans)

    w_lat = w_latent.astype(F32)
    centred = w_lat - jnp.mean(w_lat, axis=1, keepdims=True)
    gram = (
        lax.dot_general(
            centred, centred, (((1,), (1,)), ((), ())), precision=lax.Precision.HIGHEST
        )
        / width
    )
    half = chans // 2
    scaled = centred * (1.0 + shifts[1])
    pad = jnp.zeros((7, width), F32)
    left = jnp.concatenate(
        [scaled[:half], shifts[0:1], pad, scaled[half:], jnp.zeros((8, width), F32)], axis=0
    )
    left = lax.dynamic_slice_in_dim(left, seq * part, part, 1)
    stacked = jnp.concatenate(split_high(left), axis=0)
    columns = jnp.transpose(w_image_qkv, (0, 2, 1, 3)).reshape(part, heads * 3 * hd)
    partial = jnp.dot(stacked, columns, preferred_element_type=F32)
    count = left.shape[0]
    partial = partial[:count] + partial[count:]
    mine = lax.dynamic_slice_in_dim(partial, core * (count // 2), count // 2, 0)
    other = lax.dynamic_slice_in_dim(partial, (1 - core) * (count // 2), count // 2, 0)
    mine = mine + swap_cores(other)
    mine = jnp.transpose(mine.reshape(count // 2, heads, 3 * hd), (1, 0, 2))
    mine = jnp.sum(lax.all_to_all(mine, CHIPS, 0, 0, tiled=True), axis=0)
    theirs = swap_cores(mine)
    first = jnp.where(core == 0, mine, theirs)
    second = jnp.where(core == 0, theirs, mine)
    folded = jnp.concatenate([first[:half], second[:half]], axis=0)
    bias = first[half : half + 1]
    folded = jnp.concatenate([folded, gram], axis=1)
    folded = jnp.concatenate(split_high(folded), axis=0)

    w_text_other = swap_cores(w_text_mine)
    w_keys = jnp.where(core == 0, w_text_mine, w_text_other)
    w_values = jnp.where(core == 0, w_text_other, w_text_mine)
    text_in = (
        text_here.astype(F32)[None] * (1.0 + mods[:, 1][:, None]) + mods[:, 0][:, None]
    ).astype(BF16)
    text_in = text_in.reshape(-1, width)
    text_keys = rms_scale(jnp.dot(text_in, w_keys, preferred_element_type=F32), qk_gains[2])
    text_values = jnp.dot(text_in, w_values, preferred_element_type=F32)
    text_pairs = jnp.concatenate([text_keys.astype(BF16), text_values.astype(BF16)], axis=1)
    text_pairs = lax.all_to_all(
        text_pairs.reshape(steps, -1, 2 * hd), "step", 0, 0, tiled=True
    ).reshape(-1, 2 * hd)

    pair = jnp.stack([noise[0], trajectory[0]], axis=1)
    kept = lax.dynamic_index_in_dim(pair, core, 0, keepdims=False)
    came = swap_cores(lax.dynamic_index_in_dim(pair, 1 - core, 0, keepdims=False))
    own = jnp.concatenate(
        [jnp.where(core == 0, kept, came), jnp.where(core == 0, came, kept)], axis=1
    )
    own_noise, own_start = own[0], own[1]
    tokens = images * rows

    result = own_start
    for iteration in range(ITERS):
        projected = jnp.dot(latents, folded, preferred_element_type=F32)
        spread = jnp.sum(
            projected[:, 3 * hd :] * latents[:, :chans].astype(F32), axis=1, keepdims=True
        )
        projected = projected[:, : 3 * hd] * lax.rsqrt(spread + 1e-06) + bias
        queries = rms_scale(projected[:, :hd], qk_gains[0]).astype(BF16)
        image_keys = rms_scale(projected[:, hd : 2 * hd], qk_gains[1]).astype(BF16)
        image_values = projected[:, 2 * hd :].astype(BF16)
        keys = jnp.concatenate([text_pairs[:, :hd], image_keys], axis=0)
        values = jnp.concatenate([text_pairs[:, hd:], image_values], axis=0)
        scores = (
            lax.dot_general(
                queries, keys, (((1,), (1,)), ((), ())), preferred_element_type=F32
            )
            * factor
        )
        powers = jnp.exp(scores)
        probs = (powers / jnp.sum(powers, axis=-1, keepdims=True)).astype(BF16)
        attended = jnp.dot(probs, values, preferred_element_type=F32).astype(BF16)
        attended = lax.all_to_all(
            attended.reshape(chips, tokens, hd), CHIPS, 0, 0, tiled=True
        )
        attended = jnp.transpose(attended, (1, 0, 2)).reshape(tokens, heads * hd)
        mixed = lax.dot_general(
            attended, w_out, (((1,), (1,)), ((), ())), preferred_element_type=F32
        )
        mine_x = lax.dynamic_slice_in_dim(latents, chip * tokens, tokens, 0)[:, :chans]
        hidden = jnp.dot(mine_x, w_latent, preferred_element_type=F32)
        combined = hidden + shifts[2] * mixed
        final_in = (layer_norm(combined) * (1.0 + shifts[6]) + shifts[5]).astype(BF16)
        drift = jnp.dot(final_in, w_final, preferred_element_type=F32)
        increment = step_sizes[0] * drift + own_noise
        contrib = increment + jnp.where(place == 0, own_start, jnp.zeros_like(own_start))
        everyone = lax.all_to_all(
            jnp.broadcast_to(contrib[None], (steps, tokens, chans)), "step", 0, 0, tiled=True
        )
        earlier = jnp.arange(steps)[:, None, None] < place
        prefix = jnp.sum(jnp.where(earlier, everyone, 0.0), axis=0)
        result = prefix + contrib
        if iteration + 1 < ITERS:
            current = jnp.where(place == 0, own_start, prefix).astype(BF16)
            current = jnp.concatenate([current, current], axis=-1)
            latents = lax.all_to_all(
                jnp.broadcast_to(current[None], (chips, tokens, 2 * chans)),
                CHIPS,
                0,
                0,
                tiled=True,
            ).reshape(-1, 2 * chans)
    halves = result.reshape(2, rows, chans)
    kept = lax.dynamic_index_in_dim(halves, core, 0, keepdims=False)
    came = swap_cores(lax.dynamic_index_in_dim(halves, 1 - core, 0, keepdims=False))
    return jnp.stack(
        [jnp.where(core == 0, kept, came), jnp.where(core == 0, came, kept)], axis=0
    )[None]


def solution(mesh):
    steps, seq = mesh.devices.shape
    fine = Mesh(mesh.devices.reshape(steps, 4, 4, 2), ("step", "y", "x", "core"))
    placed = (
        P("step", None, SEQ, None),
        P("step", None, SEQ, None),
        P("step"),
        P("step", None, None),
        P(None, SEQ, None),
        P(),
        P(SEQ, None, None, None),
        P(SEQ, None, None, None),
        P(SEQ, None, None),
        P(),
        P(),
    )
    return jax.shard_map(
        local,
        mesh=fine,
        in_specs=placed,
        out_specs=P("step", None, SEQ, None),
        check_vma=False,
    )
```

```python
import math

import jax
import jax.numpy as jnp
from jax import lax
from jax.experimental import pallas as pl
from jax.experimental.pallas import tpu as pltpu
from jax.sharding import Mesh
from jax.sharding import PartitionSpec as P

ITERS = 2
CHIPS = ("y", "x")
SEQ = ("y", "x", "core")
F32, BF16 = jnp.float32, jnp.bfloat16
NT = (((1,), (1,)), ((), ()))
MIB = 1 << 20


def layer_norm(values):
    centre = values - jnp.mean(values, axis=-1, keepdims=True)
    spread = jnp.mean(centre * centre, axis=-1, keepdims=True)
    return centre * lax.rsqrt(spread + 1e-06)


def rms_scale(values, gains):
    return values * lax.rsqrt(jnp.mean(values * values, axis=-1, keepdims=True) + 1e-06) * gains


def split_high(values):
    high = lax.reduce_precision(values, 8, 7)
    return high.astype(BF16), (values - high).astype(BF16)


def swap_cores(values):
    return lax.ppermute(values, "core", [(0, 1), (1, 0)])


def own_half(values, core):
    kept = lax.dynamic_index_in_dim(values, core, 0, keepdims=False)
    came = swap_cores(lax.dynamic_index_in_dim(values, 1 - core, 0, keepdims=False))
    return jnp.where(core == 0, kept, came), jnp.where(core == 0, came, kept)


def attention_kernel(
    x_ref, folded_ref, gram_ref, bias_ref, gains_ref, text_ref, out_ref, q_ref, k_ref, v_ref
):
    hd = gains_ref.shape[1]
    chans = folded_ref.shape[0]
    pairs = x_ref.shape[0]
    text = text_ref.shape[0]
    chips, block, _ = out_ref.shape
    factor = math.log2(math.e) / math.sqrt(hd)
    x = x_ref[...]
    doubled = jnp.concatenate([x, x], axis=1)
    blank = jnp.zeros((chans, 4 * hd), BF16)
    k_ref[:text] = text_ref[:, :hd]
    v_ref[:text, :hd] = text_ref[:, hd:]
    v_ref[:, hd:] = jnp.ones((v_ref.shape[0], hd), BF16)
    for parity in range(2):
        weights = jnp.concatenate(
            [folded_ref[...], gram_ref[:, parity * hd : (parity + 1) * hd]], axis=1
        )
        high = weights.astype(BF16)
        low = (weights - high.astype(F32)).astype(BF16)
        rows = [high, blank, low, blank] if parity == 0 else [blank, high, blank, low]
        projected = jnp.dot(
            doubled, jnp.concatenate(rows, axis=0), preferred_element_type=F32
        )
        spread = jnp.sum(projected[:, 3 * hd :] * x.astype(F32), axis=1, keepdims=True)
        projected = projected[:, : 3 * hd] * lax.rsqrt(spread + 1e-06) + bias_ref[...]
        mine = pl.ds(parity * pairs, pairs)
        image = pl.ds(text + parity * pairs, pairs)
        q_ref[mine] = rms_scale(projected[:, :hd], gains_ref[0:1]).astype(BF16)
        k_ref[image] = rms_scale(projected[:, hd : 2 * hd], gains_ref[1:2]).astype(BF16)
        v_ref[image, :hd] = projected[:, 2 * hd :].astype(BF16)
    half = block // 2
    size = 256
    for start in range(0, 2 * pairs, size):
        scores = lax.dot_general(
            q_ref[start : start + size], k_ref[...], NT, preferred_element_type=F32
        )
        powers = jnp.exp2(scores * factor).astype(BF16)
        both = jnp.dot(powers, v_ref[...], preferred_element_type=F32)
        attended = (both[:, :hd] / both[:, hd:]).astype(BF16)
        parity, first = divmod(start, pairs)
        out_ref[first // half : (first + size) // half, parity * half : (parity + 1) * half] = (
            attended.reshape(size // half, half, hd)
        )


def attention(latents, folded, gram, bias, gains, text_pairs, chips):
    pairs = latents.shape[0]
    text, hd = text_pairs.shape[0], gains.shape[1]
    keys = text + 2 * pairs
    return pl.pallas_call(
        attention_kernel,
        out_shape=jax.ShapeDtypeStruct((chips, 2 * pairs // chips, hd), BF16),
        scratch_shapes=[
            pltpu.VMEM((2 * pairs, hd), BF16),
            pltpu.VMEM((keys, hd), BF16),
            pltpu.VMEM((keys, 2 * hd), BF16),
        ],
        compiler_params=pltpu.CompilerParams(vmem_limit_bytes=24 * MIB),
        cost_estimate=pl.CostEstimate(
            flops=8 * pairs * keys * hd, bytes_accessed=2 * MIB, transcendentals=2 * pairs * keys
        ),
        name="attention",
    )(latents, folded, gram, bias, gains, text_pairs)


def output_kernel(
    attended_ref, w_out_ref, x_ref, w_lat_ref, gate_ref, shift_ref, scale_ref, w_fin_ref,
    step_ref, added_ref, out_ref, rows_ref, mixed_ref
):
    at = pl.program_id(0)
    heads, tokens, hd = attended_ref.shape
    size = w_out_ref.shape[0]
    chans = w_lat_ref.shape[0] // 4

    @pl.when(at == 0)
    def _():
        for head in range(heads):
            rows_ref[:, head * hd : (head + 1) * hd] = attended_ref[head]

    mixed = lax.dot_general(rows_ref[...], w_out_ref[...], NT, preferred_element_type=F32)
    hidden = jnp.dot(x_ref[...], w_lat_ref[...], preferred_element_type=F32)
    mixed_ref[at] = hidden + gate_ref[...] * mixed

    @pl.when(at == pl.num_programs(0) - 1)
    def _():
        blocks = mixed_ref.shape[0]
        width = blocks * size
        total = jnp.zeros((tokens, 1), F32)
        for b in range(blocks):
            total += jnp.sum(mixed_ref[b], axis=1, keepdims=True)
        mean = total / width
        total = jnp.zeros((tokens, 1), F32)
        for b in range(blocks):
            centre = mixed_ref[b] - mean
            total += jnp.sum(centre * centre, axis=1, keepdims=True)
        scale = lax.rsqrt(total / width + 1e-06)
        half = tokens // 2
        drift = jnp.zeros((half, 2 * chans), F32)
        for b in range(blocks):
            cut = slice(b * size, (b + 1) * size)
            normal = (mixed_ref[b] - mean) * scale
            final_in = (normal * (1.0 + scale_ref[:, cut]) + shift_ref[:, cut]).astype(BF16)
            for parity in range(2):
                drift += lax.dot_general(
                    final_in[parity * half : (parity + 1) * half],
                    w_fin_ref[parity, :, cut],
                    NT,
                    preferred_element_type=F32,
                )
        contrib = step_ref[0] * drift + added_ref[...]
        out_ref[...] = jnp.broadcast_to(contrib[None], out_ref.shape)


def output_stage(attended, w_out, x, w_lat, gate, shift, scale, w_fin, step_size, added, steps):
    heads, tokens, hd = attended.shape
    width = w_out.shape[0]
    size = 512
    whole = lambda *shape: pl.BlockSpec(shape, lambda i: (0,) * len(shape))
    return pl.pallas_call(
        output_kernel,
        grid=(width // size,),
        in_specs=[
            whole(*attended.shape),
            pl.BlockSpec((size, heads * hd), lambda i: (i, 0)),
            whole(*x.shape),
            pl.BlockSpec((w_lat.shape[0], size), lambda i: (0, i)),
            pl.BlockSpec((1, size), lambda i: (0, i)),
            whole(1, width),
            whole(1, width),
            whole(*w_fin.shape),
            pl.BlockSpec(memory_space=pltpu.SMEM),
            whole(*added.shape),
        ],
        out_specs=whole(steps, *added.shape),
        out_shape=jax.ShapeDtypeStruct((steps,) + added.shape, F32),
        scratch_shapes=[
            pltpu.VMEM((tokens, heads * hd), BF16),
            pltpu.VMEM((width // size, tokens, size), F32),
        ],
        compiler_params=pltpu.CompilerParams(vmem_limit_bytes=32 * MIB),
        cost_estimate=pl.CostEstimate(
            flops=2 * tokens * width * heads * hd,
            bytes_accessed=2 * width * heads * hd,
            transcendentals=tokens,
        ),
        name="output_stage",
    )(attended, w_out, x, w_lat, gate, shift, scale, w_fin, step_size, added)


def scan_kernel(place_ref, everyone_ref, mine_ref, start_ref, out_ref, x_ref):
    place = place_ref[0]
    prefix = jnp.zeros(start_ref.shape, F32)
    for step in range(everyone_ref.shape[0]):
        prefix += jnp.where(step < place, everyone_ref[step], 0.0)
    out_ref[...] = prefix + mine_ref[0]
    current = jnp.where(place == 0, start_ref[...], prefix).astype(BF16)
    x_ref[...] = jnp.broadcast_to(current[None], x_ref.shape)


def scan(place, everyone, mine, start, chips):
    return pl.pallas_call(
        scan_kernel,
        in_specs=[pl.BlockSpec(memory_space=pltpu.SMEM)]
        + [pl.BlockSpec(memory_space=pltpu.VMEM)] * 3,
        out_shape=(
            jax.ShapeDtypeStruct(start.shape, F32),
            jax.ShapeDtypeStruct((chips,) + start.shape, BF16),
        ),
        name="scan",
    )(place, everyone, mine, start)


def local(
    trajectory,
    noise,
    step_sizes,
    modulation,
    text_states,
    w_latent,
    w_image_qkv,
    w_text_kv,
    w_out_t,
    qk_gains,
    w_final,
):
    steps = lax.axis_size("step")
    chips = lax.axis_size(CHIPS)
    place, core = lax.axis_index("step"), lax.axis_index("core")
    seq = lax.axis_index(SEQ)
    images, rows, chans = trajectory.shape[1:]
    width = w_latent.shape[1]
    part, heads, hd = w_out_t.shape
    text_rows = text_states.shape[1] // steps
    shifts = modulation[0]

    w_out_mine = w_out_t.reshape(part, heads * hd)
    mods_mine = jnp.broadcast_to(shifts[None, 3:5], (steps, 2, width))
    w_out_mine, mods_mine, text_states, w_text_kv, trajectory = lax.optimization_barrier(
        (w_out_mine, mods_mine, text_states, w_text_kv, trajectory)
    )
    w_out = lax.all_gather(w_out_mine, SEQ, tiled=True)

    mods = lax.all_to_all(mods_mine, "step", 0, 0, tiled=True)

    text_mine = lax.dynamic_slice_in_dim(text_states, place * text_rows, text_rows, 1)
    text_norm = layer_norm(text_mine.astype(F32)).astype(BF16)
    text_block = jnp.broadcast_to(
        text_norm.reshape(1, images, text_rows * width // hd, hd),
        (chips, images, text_rows * width // hd, hd),
    ).reshape(chips * images, -1, hd)
    weight_block = jnp.transpose(w_text_kv, (2, 1, 0, 3)).reshape(2 * heads, part, hd)
    start_pairs = trajectory[0].reshape(images, rows // 2, 2 * chans)
    latent_block = jnp.broadcast_to(
        start_pairs.astype(BF16)[None], (chips, images, rows // 2, 2 * chans)
    ).reshape(chips * images, rows // 2, 2 * chans)
    packed = jnp.concatenate([weight_block, text_block, latent_block], axis=1)
    (
        packed, mods, w_latent, w_image_qkv, shifts, noise, start_pairs, w_final
    ) = lax.optimization_barrier(
        (packed, mods, w_latent, w_image_qkv, shifts, noise, start_pairs, w_final)
    )
    packed = lax.all_to_all(packed, SEQ, 0, 0, tiled=True)

    w_lat = w_latent.astype(F32)
    centred = w_lat - jnp.mean(w_lat, axis=1, keepdims=True)
    gram = (
        lax.dot_general(centred, centred, NT, precision=lax.Precision.HIGHEST) / width
    )
    half = chans // 2
    scaled = centred * (1.0 + shifts[1])
    pad = jnp.zeros((7, width), F32)
    left = jnp.concatenate(
        [scaled[:half], shifts[0:1], pad, scaled[half:], jnp.zeros((8, width), F32)], axis=0
    )
    left = lax.dynamic_slice_in_dim(left, seq * part, part, 1)
    stacked = jnp.concatenate(split_high(left), axis=0)
    columns = jnp.transpose(w_image_qkv, (0, 2, 1, 3)).reshape(part, heads * 3 * hd)
    partial = jnp.dot(stacked, columns, preferred_element_type=F32)
    count = left.shape[0]
    partial = partial[:count] + partial[count:]
    mine = lax.dynamic_slice_in_dim(partial, core * (count // 2), count // 2, 0)
    other = lax.dynamic_slice_in_dim(partial, (1 - core) * (count // 2), count // 2, 0)
    mine = mine + swap_cores(other)
    mine = jnp.transpose(mine.reshape(count // 2, heads, 3 * hd), (1, 0, 2))

    noise_pairs = noise[0].reshape(images, rows // 2, 2 * chans)
    own = jnp.concatenate(
        own_half(jnp.stack([noise_pairs, start_pairs], axis=1), core), axis=1
    )
    own_noise, own_start = own[0], own[1]
    added = own_noise + jnp.where(place == 0, own_start, jnp.zeros_like(own_start))
    zeros = jnp.zeros_like(w_latent)
    w_lat_pairs = jnp.concatenate([w_latent, zeros, zeros, w_latent], axis=0)
    w_fin = jnp.swapaxes(w_final, 0, 1)
    w_fin_pairs = jnp.stack(
        [
            jnp.concatenate([w_fin, jnp.zeros_like(w_fin)], axis=0),
            jnp.concatenate([jnp.zeros_like(w_fin), w_fin], axis=0),
        ]
    )
    gram_blank = jnp.zeros((chans, 2 * chans), F32)
    gram_pairs = jnp.concatenate([gram, gram_blank, gram], axis=1)

    mine, packed = lax.optimization_barrier((mine, packed))
    mine = lax.all_to_all(mine, CHIPS, 0, 0, tiled=True)

    cut = packed.shape[1] - rows // 2
    w_text_mine = packed[:, :part].reshape(width, hd)
    text_here = packed[:, part:cut].reshape(-1, width)
    latents = packed[:, cut:].reshape(-1, 2 * chans)
    w_text_other = swap_cores(w_text_mine)
    w_keys = jnp.where(core == 0, w_text_mine, w_text_other)
    w_values = jnp.where(core == 0, w_text_other, w_text_mine)
    text_in = (
        text_here.astype(F32)[None] * (1.0 + mods[:, 1][:, None]) + mods[:, 0][:, None]
    ).astype(BF16)
    text_in = text_in.reshape(-1, width)
    text_keys = rms_scale(jnp.dot(text_in, w_keys, preferred_element_type=F32), qk_gains[2])
    text_values = jnp.dot(text_in, w_values, preferred_element_type=F32)
    text_pairs = jnp.concatenate([text_keys.astype(BF16), text_values.astype(BF16)], axis=1)
    text_pairs = text_pairs.reshape(steps, -1, 2 * hd)

    text_pairs, mine = lax.optimization_barrier((text_pairs, mine))
    text_pairs = lax.all_to_all(text_pairs, "step", 0, 0, tiled=True).reshape(-1, 2 * hd)
    mine = jnp.sum(mine, axis=0)
    theirs = swap_cores(mine)
    first = jnp.where(core == 0, mine, theirs)
    second = jnp.where(core == 0, theirs, mine)
    folded = jnp.concatenate([first[:half], second[:half]], axis=0)
    bias = first[half : half + 1]

    place_ref = place.reshape(1).astype(jnp.int32)
    x_own = own_start.astype(BF16)
    result = own_start
    for iteration in range(ITERS):
        attended = attention(latents, folded, gram_pairs, bias, qk_gains, text_pairs, chips)
        attended = lax.all_to_all(attended, CHIPS, 0, 0, tiled=True)
        blank = jnp.zeros_like(x_own)
        x_rows = jnp.concatenate(
            [
                jnp.concatenate([x_own, blank], axis=1),
                jnp.concatenate([blank, x_own], axis=1),
            ],
            axis=0,
        )
        contrib = output_stage(
            attended,
            w_out,
            x_rows,
            w_lat_pairs,
            shifts[2:3],
            shifts[5:6],
            shifts[6:7],
            w_fin_pairs,
            step_sizes,
            added,
            steps,
        )
        everyone = lax.all_to_all(contrib, "step", 0, 0, tiled=True)
        result, latents = scan(place_ref, everyone, contrib, own_start, chips)
        if iteration + 1 < ITERS:
            x_own = latents[0]
            latents = lax.all_to_all(latents, CHIPS, 0, 0, tiled=True).reshape(-1, 2 * chans)
    first, second = own_half(
        jnp.swapaxes(result.reshape(1, 2, rows // 2, 2 * chans), 0, 1), core
    )
    return jnp.concatenate([first, second], axis=0).reshape(1, images, rows, chans)


def solution(mesh):
    steps = mesh.devices.shape[0]
    fine = Mesh(mesh.devices.reshape(steps, 4, 4, 2), ("step", "y", "x", "core"))
    placed = (
        P("step", None, SEQ, None),
        P("step", None, SEQ, None),
        P("step"),
        P("step", None, None),
        P(None, SEQ, None),
        P(),
        P(SEQ, None, None, None),
        P(SEQ, None, None, None),
        P(SEQ, None, None),
        P(),
        P(),
    )
    return jax.shard_map(
        local,
        mesh=fine,
        in_specs=placed,
        out_specs=P("step", None, SEQ, None),
        check_vma=False,
    )
```

```python
import math

import jax
import jax.numpy as jnp
from jax import lax
from jax.experimental import pallas as pl
from jax.experimental.pallas import tpu as pltpu
from jax.sharding import Mesh
from jax.sharding import PartitionSpec as P

ITERS = 2
CHIPS = ("y", "x")
SEQ = ("y", "x", "core")
F32, BF16 = jnp.float32, jnp.bfloat16
NT = (((1,), (1,)), ((), ()))
MIB = 1 << 20
LANES = 128
FREE = pl.CostEstimate(flops=0, bytes_accessed=0, transcendentals=0)


def layer_norm(values):
    centre = values - jnp.mean(values, axis=-1, keepdims=True)
    spread = jnp.mean(centre * centre, axis=-1, keepdims=True)
    return centre * lax.rsqrt(spread + 1e-06)


def rms_scale(values, gains):
    return values * lax.rsqrt(jnp.mean(values * values, axis=-1, keepdims=True) + 1e-06) * gains


def swap_cores(values):
    return lax.ppermute(values, "core", [(0, 1), (1, 0)])


def own_half(values, core):
    kept = lax.dynamic_index_in_dim(values, core, 0, keepdims=False)
    came = swap_cores(lax.dynamic_index_in_dim(values, 1 - core, 0, keepdims=False))
    return jnp.where(core == 0, kept, came), jnp.where(core == 0, came, kept)


def shift_steps(values, by, steps):
    if by % steps == 0:
        return values
    return lax.ppermute(values, "step", [(i, (i + by) % steps) for i in range(steps)])


def fold_kernel(
    place_ref, shifts_ref, w_lat_ref, columns_ref, keep_ref, send_ref, gram_ref
):
    seq, core = place_ref[0], place_ref[1]
    chans, width = w_lat_ref.shape
    heads = keep_ref.shape[0]
    part, hd = columns_ref.shape[1:]
    half = chans // 2
    w_lat = w_lat_ref[...].astype(F32)
    mean = jnp.mean(w_lat, axis=1, keepdims=True)
    centred = w_lat - mean
    gram_ref[...] = (
        lax.dot_general(
            centred, centred, NT, precision=lax.Precision.HIGHEST, preferred_element_type=F32
        )
        / width
    )
    span = 2 * LANES
    first = seq * part
    base = jnp.minimum(first // LANES, (width - span) // LANES) * LANES
    window = pl.ds(pl.multiple_of(base, LANES), span)
    w_window = w_lat_ref[:, window].astype(F32) - mean
    left = jnp.concatenate(
        [
            w_window * (1.0 + shifts_ref[1:2, window]),
            shifts_ref[0:1, window],
            jnp.zeros((7, span), F32),
        ],
        axis=0,
    )
    left = pltpu.roll(left, lax.rem(span - (first - base), span), 1)[:, :part]
    count = left.shape[0]
    high = left.astype(BF16)
    low = (left - high.astype(F32)).astype(BF16)
    stacked = jnp.concatenate([high, low], axis=0)
    for head in range(heads):
        biases = []
        for kind in range(3):
            both = jnp.dot(
                stacked, columns_ref[kind * heads + head], preferred_element_type=F32
            )
            both = both[:count] + both[count:]
            rows = slice(kind * half, (kind + 1) * half)
            top, bottom = both[:half], both[half:chans]
            keep_ref[head, rows] = jnp.where(core == 0, top, bottom)
            send_ref[head, rows] = jnp.where(core == 0, bottom, top)
            biases.append(both[chans : chans + 1])
        biases = jnp.concatenate(biases + [jnp.zeros((5, hd), F32)], axis=0)
        keep_ref[head, 3 * half :] = jnp.where(core == 0, biases, 0.0)
        send_ref[head, 3 * half :] = jnp.where(core == 0, 0.0, biases)


def fold(place, shifts, w_latent, columns, heads):
    chans = w_latent.shape[0]
    hd = columns.shape[2]
    sent = jax.ShapeDtypeStruct((heads, 3 * chans // 2 + 8, hd), F32)
    return pl.pallas_call(
        fold_kernel,
        in_specs=[pl.BlockSpec(memory_space=pltpu.SMEM)]
        + [pl.BlockSpec(memory_space=pltpu.VMEM)] * 3,
        out_shape=(sent, sent, jax.ShapeDtypeStruct((chans, chans), F32)),
        compiler_params=pltpu.CompilerParams(vmem_limit_bytes=40 * MIB),
        cost_estimate=FREE,
        name="fold",
    )(place, shifts, w_latent, columns)


def sum_kernel(parts_ref, out_ref):
    total = parts_ref[0]
    for part in range(1, parts_ref.shape[0]):
        total += parts_ref[part]
    out_ref[...] = total


def sum_parts(parts):
    return pl.pallas_call(
        sum_kernel,
        out_shape=jax.ShapeDtypeStruct(parts.shape[1:], F32),
        cost_estimate=FREE,
        name="sum_parts",
    )(parts)


def text_kernel(
    place_ref, mine_ref, other_ref, mods_ref, gains_ref, out_ref, rows_ref, in_ref
):
    core = place_ref[1]
    sources = mine_ref.shape[0]
    steps, _, width = mods_ref.shape
    hd = gains_ref.shape[1]
    part = width // sources
    chunks = width // hd
    tokens = out_ref.shape[1]
    per = tokens // sources
    rows_ref[...] = mine_ref[:, part : part + per * chunks].astype(F32)
    for chunk in range(chunks):
        cut = slice(chunk * hd, (chunk + 1) * hd)
        text = jnp.concatenate(
            [rows_ref[:, row * chunks + chunk, :] for row in range(per)], axis=0
        )
        for step in range(steps):
            scale = 1.0 + mods_ref[step, 1:2, cut]
            in_ref[step * tokens : (step + 1) * tokens, cut] = (
                text * scale + mods_ref[step, 0:1, cut]
            ).astype(BF16)
    text_in = in_ref[...]
    mine = jnp.dot(
        text_in, mine_ref[:, :part].reshape(width, hd), preferred_element_type=F32
    )
    other = jnp.dot(
        text_in, other_ref[:, :part].reshape(width, hd), preferred_element_type=F32
    )
    keys = rms_scale(jnp.where(core == 0, mine, other), gains_ref[2:3]).astype(BF16)
    values = jnp.where(core == 0, other, mine).astype(BF16)
    out_ref[:, :, :hd] = keys.reshape(steps, tokens, hd)
    out_ref[:, :, hd:] = values.reshape(steps, tokens, hd)


def text_pairs_of(place, mine, other, mods, gains, tokens):
    steps, _, width = mods.shape
    sources, _, hd = mine.shape
    return pl.pallas_call(
        text_kernel,
        in_specs=[pl.BlockSpec(memory_space=pltpu.SMEM)]
        + [pl.BlockSpec(memory_space=pltpu.VMEM)] * 4,
        out_shape=jax.ShapeDtypeStruct((steps, tokens, 2 * hd), BF16),
        scratch_shapes=[
            pltpu.VMEM((sources, tokens // sources * (width // hd), hd), F32),
            pltpu.VMEM((steps * tokens, width), BF16),
        ],
        compiler_params=pltpu.CompilerParams(vmem_limit_bytes=40 * MIB),
        cost_estimate=FREE,
        name="text_pairs",
    )(place, mine, other, mods, gains)


def attention_kernel(
    place_ref, x_ref, mine_ref, theirs_ref, gram_ref, gains_ref, text_ref, out_ref,
    q_ref, k_ref, v_ref
):
    core = place_ref[1]
    hd = gains_ref.shape[1]
    chans = gram_ref.shape[0]
    half_chans = chans // 2
    pairs = x_ref.shape[0]
    text = text_ref.shape[0]
    chips, block, _ = out_ref.shape
    factor = math.log2(math.e) / math.sqrt(hd)
    x = x_ref[...]
    doubled = jnp.concatenate([x, x], axis=1)
    first = jnp.where(core == 0, mine_ref[...], theirs_ref[...])
    second = jnp.where(core == 0, theirs_ref[...], mine_ref[...])
    folded = []
    for kind in range(3):
        rows = slice(kind * half_chans, (kind + 1) * half_chans)
        folded.append(jnp.concatenate([first[rows], second[rows]], axis=0))
    bias = [first[3 * half_chans + kind : 3 * half_chans + kind + 1] for kind in range(3)]
    blank = jnp.zeros((chans, 4 * hd), BF16)
    k_ref[:text] = text_ref[:, :hd]
    v_ref[:text, :hd] = text_ref[:, hd:]
    v_ref[:, hd:] = jnp.ones((v_ref.shape[0], hd), BF16)
    none = jnp.zeros((chans, chans), F32)
    for parity in range(2):
        grams = [gram_ref[...], none] if parity == 0 else [none, gram_ref[...]]
        weights = jnp.concatenate(folded + grams, axis=1)
        high = weights.astype(BF16)
        low = (weights - high.astype(F32)).astype(BF16)
        rows = [high, blank, low, blank] if parity == 0 else [blank, high, blank, low]
        projected = jnp.dot(
            doubled, jnp.concatenate(rows, axis=0), preferred_element_type=F32
        )
        spread = jnp.sum(projected[:, 3 * hd :] * x.astype(F32), axis=1, keepdims=True)
        scale = lax.rsqrt(spread + 1e-06)
        mine = pl.ds(parity * pairs, pairs)
        image = pl.ds(text + parity * pairs, pairs)
        queries = projected[:, :hd] * scale + bias[0]
        image_keys = projected[:, hd : 2 * hd] * scale + bias[1]
        q_ref[mine] = rms_scale(queries, gains_ref[0:1]).astype(BF16)
        k_ref[image] = rms_scale(image_keys, gains_ref[1:2]).astype(BF16)
        v_ref[image, :hd] = (projected[:, 2 * hd : 3 * hd] * scale + bias[2]).astype(BF16)
    half = block // 2
    size = 256
    for start in range(0, 2 * pairs, size):
        scores = lax.dot_general(
            q_ref[start : start + size], k_ref[...], NT, preferred_element_type=F32
        )
        powers = jnp.exp2(scores * factor).astype(BF16)
        both = jnp.dot(powers, v_ref[...], preferred_element_type=F32)
        attended = (both[:, :hd] / both[:, hd:]).astype(BF16)
        parity, begin = divmod(start, pairs)
        out_ref[begin // half : (begin + size) // half, parity * half : (parity + 1) * half] = (
            attended.reshape(size // half, half, hd)
        )


def attention(place, latents, mine, theirs, gram, gains, text_pairs, chips):
    pairs = latents.shape[0]
    text, hd = text_pairs.shape[0], gains.shape[1]
    keys = text + 2 * pairs
    return pl.pallas_call(
        attention_kernel,
        in_specs=[pl.BlockSpec(memory_space=pltpu.SMEM)]
        + [pl.BlockSpec(memory_space=pltpu.VMEM)] * 6,
        out_shape=jax.ShapeDtypeStruct((chips, 2 * pairs // chips, hd), BF16),
        scratch_shapes=[
            pltpu.VMEM((2 * pairs, hd), BF16),
            pltpu.VMEM((keys, hd), BF16),
            pltpu.VMEM((keys, 2 * hd), BF16),
        ],
        compiler_params=pltpu.CompilerParams(vmem_limit_bytes=60 * MIB),
        cost_estimate=pl.CostEstimate(
            flops=8 * pairs * keys * hd, bytes_accessed=2 * MIB, transcendentals=2 * pairs * keys
        ),
        name="attention",
    )(place, latents, mine, theirs, gram, gains, text_pairs)


def output_kernel(
    attended_ref, w_out_ref, x_ref, w_lat_ref, shifts_ref, w_fin_ref, step_ref, added_ref,
    out_ref, rows_ref, w_ref, mixed_ref, sems
):
    heads, tokens, hd = attended_ref.shape
    chunks = sems.shape[0]
    chans, width = w_lat_ref.shape
    size = width // chunks
    half = tokens // 2
    copies = [
        pltpu.make_async_copy(
            w_out_ref.at[pl.ds(c * size, size)], w_ref.at[pl.ds(c * size, size)], sems.at[c]
        )
        for c in range(chunks)
    ]
    for copy in copies:
        copy.start()
    for head in range(heads):
        rows_ref[:, head * hd : (head + 1) * hd] = attended_ref[head]
    x = x_ref[...].astype(F32)
    x = jnp.concatenate([x[:, :chans], x[:, chans:]], axis=0).astype(BF16)
    total = jnp.zeros((tokens, 1), F32)
    for c in range(chunks):
        cut = slice(c * size, (c + 1) * size)
        copies[c].wait()
        mixed = lax.dot_general(rows_ref[...], w_ref[cut], NT, preferred_element_type=F32)
        hidden = jnp.dot(x, w_lat_ref[:, cut], preferred_element_type=F32)
        combined = hidden + shifts_ref[2:3, cut] * mixed
        mixed_ref[c] = combined
        total += jnp.sum(combined, axis=1, keepdims=True)
    mean = total / width
    total = jnp.zeros((tokens, 1), F32)
    for c in range(chunks):
        centre = mixed_ref[c] - mean
        total += jnp.sum(centre * centre, axis=1, keepdims=True)
    scale = lax.rsqrt(total / width + 1e-06)
    drift = jnp.zeros((tokens, chans), F32)
    for c in range(chunks):
        cut = slice(c * size, (c + 1) * size)
        normal = (mixed_ref[c] - mean) * scale
        final_in = (normal * (1.0 + shifts_ref[6:7, cut]) + shifts_ref[5:6, cut]).astype(BF16)
        drift += lax.dot_general(final_in, w_fin_ref[:, cut], NT, preferred_element_type=F32)
    drift = jnp.concatenate([drift[:half], drift[half:]], axis=1)
    contrib = step_ref[0] * drift + added_ref[...]
    out_ref[...] = jnp.broadcast_to(contrib[None], out_ref.shape)


def output_stage(attended, w_out, x, w_lat, shifts, w_fin, step_size, added, steps):
    heads, tokens, hd = attended.shape
    width = w_out.shape[0]
    chunks = 6
    vmem = pl.BlockSpec(memory_space=pltpu.VMEM)
    return pl.pallas_call(
        output_kernel,
        in_specs=[
            vmem,
            pl.BlockSpec(memory_space=pl.ANY),
            vmem,
            vmem,
            vmem,
            vmem,
            pl.BlockSpec(memory_space=pltpu.SMEM),
            vmem,
        ],
        out_shape=jax.ShapeDtypeStruct((steps,) + added.shape, F32),
        scratch_shapes=[
            pltpu.VMEM((tokens, heads * hd), BF16),
            pltpu.VMEM((width, heads * hd), BF16),
            pltpu.VMEM((chunks, tokens, width // chunks), F32),
            pltpu.SemaphoreType.DMA((chunks,)),
        ],
        compiler_params=pltpu.CompilerParams(vmem_limit_bytes=60 * MIB),
        cost_estimate=pl.CostEstimate(
            flops=2 * tokens * width * heads * hd,
            bytes_accessed=2 * width * heads * hd,
            transcendentals=tokens,
        ),
        name="output_stage",
    )(attended, w_out, x, w_lat, shifts, w_fin, step_size, added)


def scan_kernel(place_ref, everyone_ref, mine_ref, start_ref, out_ref, x_ref):
    place = place_ref[0]
    prefix = jnp.zeros(start_ref.shape, F32)
    for step in range(everyone_ref.shape[0]):
        prefix += jnp.where(step < place, everyone_ref[step], 0.0)
    out_ref[...] = prefix + mine_ref[0]
    current = jnp.where(place == 0, start_ref[...], prefix).astype(BF16)
    x_ref[...] = jnp.broadcast_to(current[None], x_ref.shape)


def scan(place, everyone, mine, start, chips):
    return pl.pallas_call(
        scan_kernel,
        in_specs=[pl.BlockSpec(memory_space=pltpu.SMEM)]
        + [pl.BlockSpec(memory_space=pltpu.VMEM)] * 3,
        out_shape=(
            jax.ShapeDtypeStruct(start.shape, F32),
            jax.ShapeDtypeStruct((chips,) + start.shape, BF16),
        ),
        name="scan",
    )(place, everyone, mine, start)


def local(
    trajectory,
    noise,
    step_sizes,
    modulation,
    text_states,
    w_latent,
    w_image_qkv,
    w_text_kv,
    w_out_t,
    qk_gains,
    w_final,
):
    steps = lax.axis_size("step")
    chips = lax.axis_size(CHIPS)
    place, core = lax.axis_index("step"), lax.axis_index("core")
    seq = lax.axis_index(SEQ)
    images, rows, chans = trajectory.shape[1:]
    width = w_latent.shape[1]
    part, heads, hd = w_out_t.shape
    text_rows = text_states.shape[1] // steps
    shifts = modulation[0]

    w_out_mine = w_out_t.reshape(part, heads * hd)
    w_out_mine, text_states, w_text_kv, trajectory, w_image_qkv = lax.optimization_barrier(
        (w_out_mine, text_states, w_text_kv, trajectory, w_image_qkv)
    )
    w_out = lax.all_gather(w_out_mine, SEQ, tiled=True)

    mods = shifts[None, 3:5]
    while mods.shape[0] < steps:
        mods = jnp.concatenate([mods, shift_steps(mods, mods.shape[0], steps)], axis=0)

    text_mine = lax.dynamic_slice_in_dim(text_states, place * text_rows, text_rows, 1)
    text_norm = layer_norm(text_mine.astype(F32)).astype(BF16)
    text_block = jnp.broadcast_to(
        text_norm.reshape(1, images, text_rows * width // hd, hd),
        (chips, images, text_rows * width // hd, hd),
    ).reshape(chips * images, -1, hd)
    weight_block = jnp.transpose(w_text_kv, (2, 1, 0, 3)).reshape(2 * heads, part, hd)
    start_pairs = trajectory[0].reshape(images, rows // 2, 2 * chans)
    latent_block = jnp.broadcast_to(
        start_pairs.astype(BF16)[None], (chips, images, rows // 2, 2 * chans)
    ).reshape(chips * images, rows // 2, 2 * chans)
    packed = jnp.concatenate([weight_block, text_block, latent_block], axis=1)
    columns = jnp.swapaxes(w_image_qkv.reshape(part, 3 * heads, hd), 0, 1)
    packed, w_latent, shifts, columns = lax.optimization_barrier(
        (packed, w_latent, shifts, columns)
    )
    packed = lax.all_to_all(packed, SEQ, 0, 0, tiled=True)

    where = jnp.stack([seq, core]).astype(jnp.int32)
    keep, send, gram = fold(where, shifts, w_latent, columns, heads)
    mine = keep + swap_cores(send)

    mine, packed, mods = lax.optimization_barrier((mine, packed, mods))
    mine = lax.all_to_all(mine, CHIPS, 0, 0, tiled=True)

    text_pairs = text_pairs_of(
        where, packed, swap_cores(packed), mods, qk_gains, text_rows * lax.axis_size(SEQ)
    )
    latents = packed[:, part + text_rows * width // hd :].reshape(-1, 2 * chans)

    text_pairs = jnp.concatenate(
        [shift_steps(text_pairs[k], -k, steps) for k in range(steps)], axis=0
    )
    mine, text_pairs, noise, start_pairs, w_final = lax.optimization_barrier(
        (mine, text_pairs, noise, start_pairs, w_final)
    )
    mine = sum_parts(mine)
    theirs = swap_cores(mine)

    noise_pairs = noise[0].reshape(images, rows // 2, 2 * chans)
    own = jnp.concatenate(
        own_half(jnp.stack([noise_pairs, start_pairs], axis=1), core), axis=1
    )
    own_noise, own_start = own[0], own[1]
    added = own_noise + jnp.where(place == 0, own_start, jnp.zeros_like(own_start))
    w_fin = jnp.swapaxes(w_final, 0, 1)

    place_ref = place.reshape(1).astype(jnp.int32)
    x_own = own_start.astype(BF16)
    result = own_start
    for iteration in range(ITERS):
        attended = attention(where, latents, mine, theirs, gram, qk_gains, text_pairs, chips)
        attended = lax.all_to_all(attended, CHIPS, 0, 0, tiled=True)
        contrib = output_stage(
            attended, w_out, x_own, w_latent, shifts, w_fin, step_sizes, added, steps
        )
        everyone = lax.all_to_all(contrib, "step", 0, 0, tiled=True)
        result, latents = scan(place_ref, everyone, contrib, own_start, chips)
        if iteration + 1 < ITERS:
            x_own = latents[0]
            latents = lax.all_to_all(latents, CHIPS, 0, 0, tiled=True).reshape(-1, 2 * chans)
    first, second = own_half(
        jnp.swapaxes(result.reshape(1, 2, rows // 2, 2 * chans), 0, 1), core
    )
    return jnp.concatenate([first, second], axis=0).reshape(1, images, rows, chans)


def solution(mesh):
    steps = mesh.devices.shape[0]
    fine = Mesh(mesh.devices.reshape(steps, 4, 4, 2), ("step", "y", "x", "core"))
    placed = (
        P("step", None, SEQ, None),
        P("step", None, SEQ, None),
        P("step"),
        P("step", None, None),
        P(None, SEQ, None),
        P(),
        P(SEQ, None, None, None),
        P(SEQ, None, None, None),
        P(SEQ, None, None),
        P(),
        P(),
    )
    return jax.shard_map(
        local,
        mesh=fine,
        in_specs=placed,
        out_specs=P("step", None, SEQ, None),
        check_vma=False,
    )
```

```python
import math

import jax
import jax.numpy as jnp
from jax import lax
from jax.experimental import pallas as pl
from jax.experimental.pallas import tpu as pltpu
from jax.sharding import Mesh
from jax.sharding import PartitionSpec as P

ITERS = 2
CHIPS = ("y", "x")
SEQ = ("y", "x", "core")
F32, BF16 = jnp.float32, jnp.bfloat16
NT = (((1,), (1,)), ((), ()))
MIB = 1 << 20
LANES = 128
VMEM_LIMIT = 28 * MIB
FREE = pl.CostEstimate(flops=0, bytes_accessed=0, transcendentals=0)


def layer_norm(values):
    centre = values - jnp.mean(values, axis=-1, keepdims=True)
    spread = jnp.mean(centre * centre, axis=-1, keepdims=True)
    return centre * lax.rsqrt(spread + 1e-06)


def rms_scale(values, gains):
    return values * lax.rsqrt(jnp.mean(values * values, axis=-1, keepdims=True) + 1e-06) * gains


def swap_cores(values):
    return lax.ppermute(values, "core", [(0, 1), (1, 0)])


def own_half(values, core):
    kept = lax.dynamic_index_in_dim(values, core, 0, keepdims=False)
    came = swap_cores(lax.dynamic_index_in_dim(values, 1 - core, 0, keepdims=False))
    return jnp.where(core == 0, kept, came), jnp.where(core == 0, came, kept)


def shift_steps(values, by, steps):
    if by % steps == 0:
        return values
    return lax.ppermute(values, "step", [(i, (i + by) % steps) for i in range(steps)])


def fold_kernel(
    place_ref, shifts_ref, w_lat_ref, columns_ref, keep_ref, send_ref, gram_ref
):
    seq, core = place_ref[0], place_ref[1]
    chans, width = w_lat_ref.shape
    heads, sent = keep_ref.shape[:2]
    part, hd = columns_ref.shape[1:]
    half = chans // 2
    w_lat = w_lat_ref[...].astype(F32)
    mean = jnp.mean(w_lat, axis=1, keepdims=True)
    centred = w_lat - mean
    gram_ref[...] = (
        lax.dot_general(
            centred, centred, NT, precision=lax.Precision.HIGHEST, preferred_element_type=F32
        )
        / width
    )
    span = 2 * LANES
    first = seq * part
    base = jnp.minimum(first // LANES, (width - span) // LANES) * LANES
    window = pl.ds(pl.multiple_of(base, LANES), span)
    w_window = w_lat_ref[:, window].astype(F32) - mean
    left = jnp.concatenate(
        [
            w_window * (1.0 + shifts_ref[1:2, window]),
            shifts_ref[0:1, window],
            jnp.zeros((7, span), F32),
        ],
        axis=0,
    )
    left = pltpu.roll(left, lax.rem(span - (first - base), span), 1)[:, :part]
    count = left.shape[0]
    high = left.astype(BF16)
    low = (left - high.astype(F32)).astype(BF16)
    stacked = jnp.concatenate([high, low], axis=0)
    for head in range(heads):
        biases = []
        for kind in range(3):
            both = jnp.dot(
                stacked, columns_ref[kind * heads + head], preferred_element_type=F32
            )
            both = both[:count] + both[count:]
            rows = slice(kind * half, (kind + 1) * half)
            top, bottom = both[:half], both[half:chans]
            keep_ref[head, rows] = jnp.where(core == 0, top, bottom)
            send_ref[head, rows] = jnp.where(core == 0, bottom, top)
            biases.append(both[chans : chans + 1])
        biases.append(jnp.zeros((sent - 3 * half - 3, hd), F32))
        biases = jnp.concatenate(biases, axis=0)
        keep_ref[head, 3 * half :] = jnp.where(core == 0, biases, 0.0)
        send_ref[head, 3 * half :] = jnp.where(core == 0, 0.0, biases)


def fold(place, shifts, w_latent, columns, heads):
    chans = w_latent.shape[0]
    hd = columns.shape[2]
    sent = jax.ShapeDtypeStruct((heads, 3 * chans // 2 + 16, hd), F32)
    return pl.pallas_call(
        fold_kernel,
        in_specs=[pl.BlockSpec(memory_space=pltpu.SMEM)]
        + [pl.BlockSpec(memory_space=pltpu.VMEM)] * 3,
        out_shape=(sent, sent, jax.ShapeDtypeStruct((chans, chans), F32)),
        compiler_params=pltpu.CompilerParams(vmem_limit_bytes=24 * MIB),
        cost_estimate=FREE,
        name="fold",
    )(place, shifts, w_latent, columns)


def add_kernel(one_ref, other_ref, out_ref):
    out_ref[...] = (one_ref[...] + other_ref[...]).astype(BF16)


def add_parts(one, other):
    return pl.pallas_call(
        add_kernel,
        out_shape=jax.ShapeDtypeStruct(one.shape, BF16),
        cost_estimate=FREE,
        name="add_parts",
    )(one, other)


def sum_kernel(parts_ref, out_ref):
    total = parts_ref[0].astype(F32)
    for part in range(1, parts_ref.shape[0]):
        total += parts_ref[part].astype(F32)
    out_ref[...] = total


def sum_parts(parts):
    return pl.pallas_call(
        sum_kernel,
        out_shape=jax.ShapeDtypeStruct(parts.shape[1:], F32),
        cost_estimate=FREE,
        name="sum_parts",
    )(parts)


def text_kernel(
    place_ref, mine_ref, other_ref, mods_ref, gains_ref, out_ref, rows_ref, in_ref
):
    core = place_ref[1]
    sources = mine_ref.shape[0]
    steps, _, width = mods_ref.shape
    hd = gains_ref.shape[1]
    part = width // sources
    chunks = width // hd
    tokens = out_ref.shape[1]
    per = tokens // sources
    rows_ref[...] = mine_ref[:, part : part + per * chunks].astype(F32)
    for chunk in range(chunks):
        cut = slice(chunk * hd, (chunk + 1) * hd)
        text = jnp.concatenate(
            [rows_ref[:, row * chunks + chunk, :] for row in range(per)], axis=0
        )
        for step in range(steps):
            scale = 1.0 + mods_ref[step, 1:2, cut]
            in_ref[step * tokens : (step + 1) * tokens, cut] = (
                text * scale + mods_ref[step, 0:1, cut]
            ).astype(BF16)
    text_in = in_ref[...]
    mine = jnp.dot(
        text_in, mine_ref[:, :part].reshape(width, hd), preferred_element_type=F32
    )
    other = jnp.dot(
        text_in, other_ref[:, :part].reshape(width, hd), preferred_element_type=F32
    )
    keys = rms_scale(jnp.where(core == 0, mine, other), gains_ref[2:3]).astype(BF16)
    values = jnp.where(core == 0, other, mine).astype(BF16)
    out_ref[:, :, :hd] = keys.reshape(steps, tokens, hd)
    out_ref[:, :, hd:] = values.reshape(steps, tokens, hd)


def text_pairs_of(place, mine, other, mods, gains, tokens):
    steps, _, width = mods.shape
    sources, _, hd = mine.shape
    return pl.pallas_call(
        text_kernel,
        in_specs=[pl.BlockSpec(memory_space=pltpu.SMEM)]
        + [pl.BlockSpec(memory_space=pltpu.VMEM)] * 4,
        out_shape=jax.ShapeDtypeStruct((steps, tokens, 2 * hd), BF16),
        scratch_shapes=[
            pltpu.VMEM((sources, tokens // sources * (width // hd), hd), F32),
            pltpu.VMEM((steps * tokens, width), BF16),
        ],
        compiler_params=pltpu.CompilerParams(vmem_limit_bytes=24 * MIB),
        cost_estimate=FREE,
        name="text_pairs",
    )(place, mine, other, mods, gains)


def attention_kernel(
    place_ref, x_ref, mine_ref, theirs_ref, gram_ref, gains_ref, text_ref, out_ref,
    q_ref, k_ref, v_ref
):
    core = place_ref[1]
    hd = gains_ref.shape[1]
    chans = gram_ref.shape[0]
    half_chans = chans // 2
    pairs = x_ref.shape[0]
    text = text_ref.shape[0]
    chips, block, _ = out_ref.shape
    factor = math.log2(math.e) / math.sqrt(hd)
    x = x_ref[...]
    doubled = jnp.concatenate([x, x], axis=1)
    first = jnp.where(core == 0, mine_ref[...], theirs_ref[...])
    second = jnp.where(core == 0, theirs_ref[...], mine_ref[...])
    folded = []
    for kind in range(3):
        rows = slice(kind * half_chans, (kind + 1) * half_chans)
        folded.append(jnp.concatenate([first[rows], second[rows]], axis=0))
    bias = [first[3 * half_chans + kind : 3 * half_chans + kind + 1] for kind in range(3)]
    blank = jnp.zeros((chans, 4 * hd), BF16)
    k_ref[:text] = text_ref[:, :hd]
    v_ref[:text, :hd] = text_ref[:, hd:]
    v_ref[:, hd:] = jnp.ones((v_ref.shape[0], hd), BF16)
    none = jnp.zeros((chans, chans), F32)
    for parity in range(2):
        grams = [gram_ref[...], none] if parity == 0 else [none, gram_ref[...]]
        weights = jnp.concatenate(folded + grams, axis=1)
        high = weights.astype(BF16)
        low = (weights - high.astype(F32)).astype(BF16)
        rows = [high, blank, low, blank] if parity == 0 else [blank, high, blank, low]
        projected = jnp.dot(
            doubled, jnp.concatenate(rows, axis=0), preferred_element_type=F32
        )
        spread = jnp.sum(projected[:, 3 * hd :] * x.astype(F32), axis=1, keepdims=True)
        scale = lax.rsqrt(spread + 1e-06)
        mine = pl.ds(parity * pairs, pairs)
        image = pl.ds(text + parity * pairs, pairs)
        queries = projected[:, :hd] * scale + bias[0]
        image_keys = projected[:, hd : 2 * hd] * scale + bias[1]
        q_ref[mine] = rms_scale(queries, gains_ref[0:1]).astype(BF16)
        k_ref[image] = rms_scale(image_keys, gains_ref[1:2]).astype(BF16)
        v_ref[image, :hd] = (projected[:, 2 * hd : 3 * hd] * scale + bias[2]).astype(BF16)
    half = block // 2
    size = 256
    for start in range(0, 2 * pairs, size):
        scores = lax.dot_general(
            q_ref[start : start + size], k_ref[...], NT, preferred_element_type=F32
        )
        powers = jnp.exp2(scores * factor).astype(BF16)
        both = jnp.dot(powers, v_ref[...], preferred_element_type=F32)
        attended = (both[:, :hd] / both[:, hd:]).astype(BF16)
        parity, begin = divmod(start, pairs)
        out_ref[begin // half : (begin + size) // half, parity * half : (parity + 1) * half] = (
            attended.reshape(size // half, half, hd)
        )


def attention(place, latents, mine, theirs, gram, gains, text_pairs, chips):
    pairs = latents.shape[0]
    text, hd = text_pairs.shape[0], gains.shape[1]
    keys = text + 2 * pairs
    return pl.pallas_call(
        attention_kernel,
        in_specs=[pl.BlockSpec(memory_space=pltpu.SMEM)]
        + [pl.BlockSpec(memory_space=pltpu.VMEM)] * 6,
        out_shape=jax.ShapeDtypeStruct((chips, 2 * pairs // chips, hd), BF16),
        scratch_shapes=[
            pltpu.VMEM((2 * pairs, hd), BF16),
            pltpu.VMEM((keys, hd), BF16),
            pltpu.VMEM((keys, 2 * hd), BF16),
        ],
        compiler_params=pltpu.CompilerParams(vmem_limit_bytes=VMEM_LIMIT),
        cost_estimate=pl.CostEstimate(
            flops=8 * pairs * keys * hd, bytes_accessed=2 * MIB, transcendentals=2 * pairs * keys
        ),
        name="attention",
    )(place, latents, mine, theirs, gram, gains, text_pairs)


def output_kernel(
    attended_ref, w_out_ref, x_ref, w_lat_ref, shifts_ref, w_fin_ref, step_ref, added_ref,
    out_ref, rows_ref, mixed_ref
):
    heads, tokens, hd = attended_ref.shape
    chunks = mixed_ref.shape[0]
    chans, width = w_lat_ref.shape
    size = width // chunks
    half = tokens // 2
    for head in range(heads):
        rows_ref[:, head * hd : (head + 1) * hd] = attended_ref[head]
    x = x_ref[...].astype(F32)
    x = jnp.concatenate([x[:, :chans], x[:, chans:]], axis=0).astype(BF16)
    total = jnp.zeros((tokens, 1), F32)
    for c in range(chunks):
        cut = slice(c * size, (c + 1) * size)
        mixed = lax.dot_general(rows_ref[...], w_out_ref[cut], NT, preferred_element_type=F32)
        hidden = jnp.dot(x, w_lat_ref[:, cut], preferred_element_type=F32)
        combined = hidden + shifts_ref[2:3, cut] * mixed
        mixed_ref[c] = combined
        total += jnp.sum(combined, axis=1, keepdims=True)
    mean = total / width
    total = jnp.zeros((tokens, 1), F32)
    for c in range(chunks):
        centre = mixed_ref[c] - mean
        total += jnp.sum(centre * centre, axis=1, keepdims=True)
    scale = lax.rsqrt(total / width + 1e-06)
    drift = jnp.zeros((tokens, chans), F32)
    for c in range(chunks):
        cut = slice(c * size, (c + 1) * size)
        normal = (mixed_ref[c] - mean) * scale
        final_in = (normal * (1.0 + shifts_ref[6:7, cut]) + shifts_ref[5:6, cut]).astype(BF16)
        drift += lax.dot_general(final_in, w_fin_ref[:, cut], NT, preferred_element_type=F32)
    drift = jnp.concatenate([drift[:half], drift[half:]], axis=1)
    contrib = step_ref[0] * drift + added_ref[...]
    out_ref[...] = jnp.broadcast_to(contrib[None], out_ref.shape)


def output_stage(attended, w_out, x, w_lat, shifts, w_fin, step_size, added, steps):
    heads, tokens, hd = attended.shape
    width = w_out.shape[0]
    chunks = 6
    vmem = pl.BlockSpec(memory_space=pltpu.VMEM)
    return pl.pallas_call(
        output_kernel,
        in_specs=[
            vmem,
            vmem,
            vmem,
            vmem,
            vmem,
            vmem,
            pl.BlockSpec(memory_space=pltpu.SMEM),
            vmem,
        ],
        out_shape=jax.ShapeDtypeStruct((steps,) + added.shape, F32),
        scratch_shapes=[
            pltpu.VMEM((tokens, heads * hd), BF16),
            pltpu.VMEM((chunks, tokens, width // chunks), F32),
        ],
        compiler_params=pltpu.CompilerParams(vmem_limit_bytes=VMEM_LIMIT),
        cost_estimate=pl.CostEstimate(
            flops=2 * tokens * width * heads * hd,
            bytes_accessed=2 * width * heads * hd,
            transcendentals=tokens,
        ),
        name="output_stage",
    )(attended, w_out, x, w_lat, shifts, w_fin, step_size, added)


def prefix_of(place, everyone_ref):
    prefix = jnp.zeros(everyone_ref.shape[1:], F32)
    for step in range(everyone_ref.shape[0]):
        prefix += jnp.where(step < place, everyone_ref[step], 0.0)
    return prefix


def scan_kernel(place_ref, everyone_ref, start_ref, x_ref):
    place = place_ref[2]
    current = jnp.where(place == 0, start_ref[...], prefix_of(place, everyone_ref))
    x_ref[...] = jnp.broadcast_to(current.astype(BF16)[None], x_ref.shape)


def scan(place, everyone, start, chips):
    return pl.pallas_call(
        scan_kernel,
        in_specs=[pl.BlockSpec(memory_space=pltpu.SMEM)]
        + [pl.BlockSpec(memory_space=pltpu.VMEM)] * 2,
        out_shape=jax.ShapeDtypeStruct((chips,) + start.shape, BF16),
        name="scan",
    )(place, everyone, start)


def total_kernel(place_ref, everyone_ref, mine_ref, keep_ref, send_ref):
    core, place = place_ref[1], place_ref[2]
    total = prefix_of(place, everyone_ref) + mine_ref[0]
    half, chans = total.shape[0] // 2, keep_ref.shape[1]
    top, bottom = total[:half], total[half:]
    for ref, pairs in (
        (keep_ref, jnp.where(core == 0, top, bottom)),
        (send_ref, jnp.where(core == 0, bottom, top)),
    ):
        ref[pl.ds(0, half, stride=2), :] = pairs[:, :chans]
        ref[pl.ds(1, half, stride=2), :] = pairs[:, chans:]


def total_rows(place, everyone, mine, rows, chans):
    half = jax.ShapeDtypeStruct((rows, chans), F32)
    return pl.pallas_call(
        total_kernel,
        in_specs=[pl.BlockSpec(memory_space=pltpu.SMEM)]
        + [pl.BlockSpec(memory_space=pltpu.VMEM)] * 2,
        out_shape=(half, half),
        name="total_rows",
    )(place, everyone, mine)


def local(
    trajectory,
    noise,
    step_sizes,
    modulation,
    text_states,
    w_latent,
    w_image_qkv,
    w_text_kv,
    w_out_t,
    qk_gains,
    w_final,
):
    steps = lax.axis_size("step")
    chips = lax.axis_size(CHIPS)
    place, core = lax.axis_index("step"), lax.axis_index("core")
    seq = lax.axis_index(SEQ)
    images, rows, chans = trajectory.shape[1:]
    width = w_latent.shape[1]
    part, heads, hd = w_out_t.shape
    text_rows = text_states.shape[1] // steps
    shifts = modulation[0]

    w_out_mine = w_out_t.reshape(part, heads * hd)
    w_out_mine, text_states, w_text_kv, trajectory, w_image_qkv = lax.optimization_barrier(
        (w_out_mine, text_states, w_text_kv, trajectory, w_image_qkv)
    )
    mods = shifts[None, 3:5]
    back = shift_steps(mods, 1, steps)
    near = jnp.concatenate([mods, back])
    back = shift_steps(near, 2, steps)
    ahead = shift_steps(near, -2, steps)
    across = shift_steps(near, 4, steps)
    mods = jnp.concatenate([near, back, across, ahead])

    text_mine = lax.dynamic_slice_in_dim(text_states, place * text_rows, text_rows, 1)
    text_norm = layer_norm(text_mine.astype(F32)).astype(BF16)
    text_block = jnp.broadcast_to(
        text_norm.reshape(1, images, text_rows * width // hd, hd),
        (chips, images, text_rows * width // hd, hd),
    ).reshape(chips * images, -1, hd)
    weight_block = jnp.transpose(w_text_kv, (2, 1, 0, 3)).reshape(2 * heads, part, hd)
    start_pairs = trajectory[0].reshape(images, rows // 2, 2 * chans)
    latent_block = jnp.broadcast_to(
        start_pairs.astype(BF16)[None], (chips, images, rows // 2, 2 * chans)
    ).reshape(chips * images, rows // 2, 2 * chans)
    packed = jnp.concatenate([weight_block, text_block, latent_block], axis=1)
    columns = jnp.swapaxes(w_image_qkv.reshape(part, 3 * heads, hd), 0, 1)
    packed, w_latent, shifts, columns, w_out_mine = lax.optimization_barrier(
        (packed, w_latent, shifts, columns, w_out_mine)
    )
    w_out = lax.all_gather(w_out_mine, SEQ, tiled=True)
    packed = lax.all_to_all(packed, SEQ, 0, 0, tiled=True)

    where = jnp.stack([seq, core, place]).astype(jnp.int32)
    keep, send, gram = fold(where, shifts, w_latent, columns, heads)
    mine = add_parts(keep, swap_cores(send))

    mine, packed, mods = lax.optimization_barrier((mine, packed, mods))
    mine = lax.all_to_all(mine, CHIPS, 0, 0, tiled=True)

    text_pairs = text_pairs_of(
        where, packed, swap_cores(packed), mods, qk_gains, text_rows * lax.axis_size(SEQ)
    )
    latents = packed[:, part + text_rows * width // hd :].reshape(-1, 2 * chans)

    received = [shift_steps(text_pairs[k], -k, steps) for k in (0, 1, 7, 2, 6, 3, 5, 4)]
    mine, received[:4], noise, start_pairs, w_final = lax.optimization_barrier(
        (mine, received[:4], noise, start_pairs, w_final)
    )
    text_pairs = jnp.concatenate(received, axis=0)
    mine = sum_parts(mine)
    theirs = swap_cores(mine)

    noise_pairs = noise[0].reshape(images, rows // 2, 2 * chans)
    own = jnp.concatenate(
        own_half(jnp.stack([noise_pairs, start_pairs], axis=1), core), axis=1
    )
    own_noise, own_start = own[0], own[1]
    added = own_noise + jnp.where(place == 0, own_start, jnp.zeros_like(own_start))
    w_fin = jnp.swapaxes(w_final, 0, 1)

    x_own = own_start.astype(BF16)
    for iteration in range(ITERS):
        attended = attention(where, latents, mine, theirs, gram, qk_gains, text_pairs, chips)
        attended = lax.all_to_all(attended, CHIPS, 0, 0, tiled=True)
        contrib = output_stage(
            attended, w_out, x_own, w_latent, shifts, w_fin, step_sizes, added, steps
        )
        everyone = lax.all_to_all(contrib, "step", 0, 0, tiled=True)
        if iteration + 1 < ITERS:
            latents = scan(where, everyone, own_start, chips)
            x_own = latents[0]
            latents = lax.all_to_all(latents, CHIPS, 0, 0, tiled=True).reshape(-1, 2 * chans)
    kept, sent = total_rows(where, everyone, contrib, rows, chans)
    came = swap_cores(sent)
    return jnp.where(core == 0, jnp.stack([kept, came]), jnp.stack([came, kept]))[None]


def solution(mesh):
    steps = mesh.devices.shape[0]
    fine = Mesh(mesh.devices.reshape(steps, 4, 4, 2), ("step", "y", "x", "core"))
    placed = (
        P("step", None, SEQ, None),
        P("step", None, SEQ, None),
        P("step"),
        P("step", None, None),
        P(None, SEQ, None),
        P(),
        P(SEQ, None, None, None),
        P(SEQ, None, None, None),
        P(SEQ, None, None),
        P(),
        P(),
    )
    return jax.shard_map(
        local,
        mesh=fine,
        in_specs=placed,
        out_specs=P("step", None, SEQ, None),
        check_vma=False,
    )
```

```python
import math

import jax
import jax.numpy as jnp
from jax import lax
from jax.experimental import pallas as pl
from jax.experimental.pallas import tpu as pltpu
from jax.sharding import Mesh
from jax.sharding import PartitionSpec as P

ITERS = 2
CHIPS = ("y", "x")
SEQ = ("y", "x", "core")
F32, BF16 = jnp.float32, jnp.bfloat16
NT = (((1,), (1,)), ((), ()))
MIB = 1 << 20
LANES = 128
VMEM_LIMIT = 28 * MIB
FREE = pl.CostEstimate(flops=0, bytes_accessed=0, transcendentals=0)


def layer_norm(values):
    centre = values - jnp.mean(values, axis=-1, keepdims=True)
    spread = jnp.mean(centre * centre, axis=-1, keepdims=True)
    return centre * lax.rsqrt(spread + 1e-06)


def rms_scale(values, gains):
    return values * lax.rsqrt(jnp.mean(values * values, axis=-1, keepdims=True) + 1e-06) * gains


def swap_cores(values):
    return lax.ppermute(values, "core", [(0, 1), (1, 0)])


def own_half(values, core):
    kept = lax.dynamic_index_in_dim(values, core, 0, keepdims=False)
    came = swap_cores(lax.dynamic_index_in_dim(values, 1 - core, 0, keepdims=False))
    return jnp.where(core == 0, kept, came), jnp.where(core == 0, came, kept)


def shift_steps(values, by, steps):
    if by % steps == 0:
        return values
    return lax.ppermute(values, "step", [(i, (i + by) % steps) for i in range(steps)])


def fold_kernel(
    place_ref, shifts_ref, w_lat_ref, columns_ref, keep_ref, send_ref, gram_ref
):
    seq, core = place_ref[0], place_ref[1]
    chans, width = w_lat_ref.shape
    heads, sent = keep_ref.shape[:2]
    part, hd = columns_ref.shape[1:]
    half = chans // 2
    w_lat = w_lat_ref[...].astype(F32)
    mean = jnp.mean(w_lat, axis=1, keepdims=True)
    centred = w_lat - mean
    gram_ref[...] = (
        lax.dot_general(
            centred, centred, NT, precision=lax.Precision.HIGHEST, preferred_element_type=F32
        )
        / width
    )
    span = 2 * LANES
    first = seq * part
    base = jnp.minimum(first // LANES, (width - span) // LANES) * LANES
    window = pl.ds(pl.multiple_of(base, LANES), span)
    w_window = w_lat_ref[:, window].astype(F32) - mean
    left = jnp.concatenate(
        [
            w_window * (1.0 + shifts_ref[1:2, window]),
            shifts_ref[0:1, window],
            jnp.zeros((7, span), F32),
        ],
        axis=0,
    )
    left = pltpu.roll(left, lax.rem(span - (first - base), span), 1)[:, :part]
    count = left.shape[0]
    high = left.astype(BF16)
    low = (left - high.astype(F32)).astype(BF16)
    stacked = jnp.concatenate([high, low], axis=0)
    for head in range(heads):
        biases = []
        for kind in range(3):
            both = jnp.dot(
                stacked, columns_ref[kind * heads + head], preferred_element_type=F32
            )
            both = both[:count] + both[count:]
            rows = slice(kind * half, (kind + 1) * half)
            top, bottom = both[:half], both[half:chans]
            keep_ref[head, rows] = jnp.where(core == 0, top, bottom)
            send_ref[head, rows] = jnp.where(core == 0, bottom, top)
            biases.append(both[chans : chans + 1])
        biases.append(jnp.zeros((sent - 3 * half - 3, hd), F32))
        biases = jnp.concatenate(biases, axis=0)
        keep_ref[head, 3 * half :] = jnp.where(core == 0, biases, 0.0)
        send_ref[head, 3 * half :] = jnp.where(core == 0, 0.0, biases)


def fold(place, shifts, w_latent, columns, heads):
    chans = w_latent.shape[0]
    hd = columns.shape[2]
    sent = jax.ShapeDtypeStruct((heads, 3 * chans // 2 + 16, hd), F32)
    return pl.pallas_call(
        fold_kernel,
        in_specs=[pl.BlockSpec(memory_space=pltpu.SMEM)]
        + [pl.BlockSpec(memory_space=pltpu.VMEM)] * 3,
        out_shape=(sent, sent, jax.ShapeDtypeStruct((chans, chans), F32)),
        compiler_params=pltpu.CompilerParams(vmem_limit_bytes=24 * MIB),
        cost_estimate=FREE,
        name="fold",
    )(place, shifts, w_latent, columns)


def add_kernel(one_ref, other_ref, out_ref):
    out_ref[...] = (one_ref[...] + other_ref[...]).astype(BF16)


def add_parts(one, other):
    return pl.pallas_call(
        add_kernel,
        out_shape=jax.ShapeDtypeStruct(one.shape, BF16),
        compiler_params=pltpu.CompilerParams(vmem_limit_bytes=8 * MIB),
        cost_estimate=FREE,
        name="add_parts",
    )(one, other)


def sum_kernel(parts_ref, out_ref):
    total = parts_ref[0].astype(F32)
    for part in range(1, parts_ref.shape[0]):
        total += parts_ref[part].astype(F32)
    out_ref[...] = total


def sum_parts(parts):
    return pl.pallas_call(
        sum_kernel,
        out_shape=jax.ShapeDtypeStruct(parts.shape[1:], F32),
        compiler_params=pltpu.CompilerParams(vmem_limit_bytes=8 * MIB),
        cost_estimate=FREE,
        name="sum_parts",
    )(parts)


def text_kernel(
    place_ref, mine_ref, other_ref, mods_ref, gains_ref, out_ref, rows_ref, in_ref
):
    core = place_ref[1]
    sources = mine_ref.shape[0]
    steps, _, width = mods_ref.shape
    hd = gains_ref.shape[1]
    part = width // sources
    chunks = width // hd
    tokens = out_ref.shape[1]
    per = tokens // sources
    rows_ref[...] = mine_ref[:, part : part + per * chunks].astype(F32)
    for chunk in range(chunks):
        cut = slice(chunk * hd, (chunk + 1) * hd)
        text = jnp.concatenate(
            [rows_ref[:, row * chunks + chunk, :] for row in range(per)], axis=0
        )
        for step in range(steps):
            scale = 1.0 + mods_ref[step, 1:2, cut]
            in_ref[step * tokens : (step + 1) * tokens, cut] = (
                text * scale + mods_ref[step, 0:1, cut]
            ).astype(BF16)
    text_in = in_ref[...]
    mine = jnp.dot(
        text_in, mine_ref[:, :part].reshape(width, hd), preferred_element_type=F32
    )
    other = jnp.dot(
        text_in, other_ref[:, :part].reshape(width, hd), preferred_element_type=F32
    )
    keys = rms_scale(jnp.where(core == 0, mine, other), gains_ref[2:3]).astype(BF16)
    values = jnp.where(core == 0, other, mine).astype(BF16)
    out_ref[:, :, :hd] = keys.reshape(steps, tokens, hd)
    out_ref[:, :, hd:] = values.reshape(steps, tokens, hd)


def text_pairs_of(place, mine, other, mods, gains, tokens):
    steps, _, width = mods.shape
    sources, _, hd = mine.shape
    return pl.pallas_call(
        text_kernel,
        in_specs=[pl.BlockSpec(memory_space=pltpu.SMEM)]
        + [pl.BlockSpec(memory_space=pltpu.VMEM)] * 4,
        out_shape=jax.ShapeDtypeStruct((steps, tokens, 2 * hd), BF16),
        scratch_shapes=[
            pltpu.VMEM((sources, tokens // sources * (width // hd), hd), F32),
            pltpu.VMEM((steps * tokens, width), BF16),
        ],
        compiler_params=pltpu.CompilerParams(vmem_limit_bytes=24 * MIB),
        cost_estimate=FREE,
        name="text_pairs",
    )(place, mine, other, mods, gains)


def attention_kernel(
    place_ref, x_ref, mine_ref, theirs_ref, gram_ref, gains_ref, text_ref, out_ref,
    q_ref, k_ref, v_ref
):
    core = place_ref[1]
    hd = gains_ref.shape[1]
    chans = gram_ref.shape[0]
    half_chans = chans // 2
    pairs = x_ref.shape[0]
    text = text_ref.shape[0]
    chips, block, _ = out_ref.shape
    factor = math.log2(math.e) / math.sqrt(hd)
    x = x_ref[...]
    doubled = jnp.concatenate([x, x], axis=1)
    first = jnp.where(core == 0, mine_ref[...], theirs_ref[...])
    second = jnp.where(core == 0, theirs_ref[...], mine_ref[...])
    folded = []
    for kind in range(3):
        rows = slice(kind * half_chans, (kind + 1) * half_chans)
        folded.append(jnp.concatenate([first[rows], second[rows]], axis=0))
    bias = [first[3 * half_chans + kind : 3 * half_chans + kind + 1] for kind in range(3)]
    blank = jnp.zeros((chans, 4 * hd), BF16)
    k_ref[:text] = text_ref[:, :hd]
    v_ref[:text, :hd] = text_ref[:, hd:]
    v_ref[:, hd:] = jnp.ones((v_ref.shape[0], hd), BF16)
    none = jnp.zeros((chans, chans), F32)
    for parity in range(2):
        grams = [gram_ref[...], none] if parity == 0 else [none, gram_ref[...]]
        weights = jnp.concatenate(folded + grams, axis=1)
        high = weights.astype(BF16)
        low = (weights - high.astype(F32)).astype(BF16)
        rows = [high, blank, low, blank] if parity == 0 else [blank, high, blank, low]
        projected = jnp.dot(
            doubled, jnp.concatenate(rows, axis=0), preferred_element_type=F32
        )
        spread = jnp.sum(projected[:, 3 * hd :] * x.astype(F32), axis=1, keepdims=True)
        scale = lax.rsqrt(spread + 1e-06)
        mine = pl.ds(parity * pairs, pairs)
        image = pl.ds(text + parity * pairs, pairs)
        queries = projected[:, :hd] * scale + bias[0]
        image_keys = projected[:, hd : 2 * hd] * scale + bias[1]
        q_ref[mine] = rms_scale(queries, gains_ref[0:1]).astype(BF16)
        k_ref[image] = rms_scale(image_keys, gains_ref[1:2]).astype(BF16)
        v_ref[image, :hd] = (projected[:, 2 * hd : 3 * hd] * scale + bias[2]).astype(BF16)
    half = block // 2
    size = 256
    for start in range(0, 2 * pairs, size):
        scores = lax.dot_general(
            q_ref[start : start + size], k_ref[...], NT, preferred_element_type=F32
        )
        powers = jnp.exp2(scores * factor).astype(BF16)
        both = jnp.dot(powers, v_ref[...], preferred_element_type=F32)
        attended = (both[:, :hd] / both[:, hd:]).astype(BF16)
        parity, begin = divmod(start, pairs)
        out_ref[begin // half : (begin + size) // half, parity * half : (parity + 1) * half] = (
            attended.reshape(size // half, half, hd)
        )


def attention(place, latents, mine, theirs, gram, gains, text_pairs, chips):
    pairs = latents.shape[0]
    text, hd = text_pairs.shape[0], gains.shape[1]
    keys = text + 2 * pairs
    return pl.pallas_call(
        attention_kernel,
        in_specs=[pl.BlockSpec(memory_space=pltpu.SMEM)]
        + [pl.BlockSpec(memory_space=pltpu.VMEM)] * 6,
        out_shape=jax.ShapeDtypeStruct((chips, 2 * pairs // chips, hd), BF16),
        scratch_shapes=[
            pltpu.VMEM((2 * pairs, hd), BF16),
            pltpu.VMEM((keys, hd), BF16),
            pltpu.VMEM((keys, 2 * hd), BF16),
        ],
        compiler_params=pltpu.CompilerParams(vmem_limit_bytes=VMEM_LIMIT),
        cost_estimate=pl.CostEstimate(
            flops=8 * pairs * keys * hd, bytes_accessed=2 * MIB, transcendentals=2 * pairs * keys
        ),
        name="attention",
    )(place, latents, mine, theirs, gram, gains, text_pairs)


def output_kernel(
    attended_ref, w_out_ref, x_ref, w_lat_ref, shifts_ref, w_fin_ref, step_ref, added_ref,
    out_ref, rows_ref, mixed_ref
):
    heads, tokens, hd = attended_ref.shape
    chunks = mixed_ref.shape[0]
    chans, width = w_lat_ref.shape
    size = width // chunks
    half = tokens // 2
    for head in range(heads):
        rows_ref[:, head * hd : (head + 1) * hd] = attended_ref[head]
    x = x_ref[...].astype(F32)
    x = jnp.concatenate([x[:, :chans], x[:, chans:]], axis=0).astype(BF16)
    total = jnp.zeros((tokens, 1), F32)
    for c in range(chunks):
        cut = slice(c * size, (c + 1) * size)
        mixed = lax.dot_general(rows_ref[...], w_out_ref[cut], NT, preferred_element_type=F32)
        hidden = jnp.dot(x, w_lat_ref[:, cut], preferred_element_type=F32)
        combined = hidden + shifts_ref[2:3, cut] * mixed
        mixed_ref[c] = combined
        total += jnp.sum(combined, axis=1, keepdims=True)
    mean = total / width
    total = jnp.zeros((tokens, 1), F32)
    for c in range(chunks):
        centre = mixed_ref[c] - mean
        total += jnp.sum(centre * centre, axis=1, keepdims=True)
    scale = lax.rsqrt(total / width + 1e-06)
    drift = jnp.zeros((tokens, chans), F32)
    for c in range(chunks):
        cut = slice(c * size, (c + 1) * size)
        normal = (mixed_ref[c] - mean) * scale
        final_in = (normal * (1.0 + shifts_ref[6:7, cut]) + shifts_ref[5:6, cut]).astype(BF16)
        drift += lax.dot_general(final_in, w_fin_ref[:, cut], NT, preferred_element_type=F32)
    drift = jnp.concatenate([drift[:half], drift[half:]], axis=1)
    contrib = step_ref[0] * drift + added_ref[...]
    out_ref[...] = jnp.broadcast_to(contrib[None], out_ref.shape)


def output_stage(attended, w_out, x, w_lat, shifts, w_fin, step_size, added, steps):
    heads, tokens, hd = attended.shape
    width = w_out.shape[0]
    chunks = 6
    vmem = pl.BlockSpec(memory_space=pltpu.VMEM)
    return pl.pallas_call(
        output_kernel,
        in_specs=[
            vmem,
            vmem,
            vmem,
            vmem,
            vmem,
            vmem,
            pl.BlockSpec(memory_space=pltpu.SMEM),
            vmem,
        ],
        out_shape=jax.ShapeDtypeStruct((steps,) + added.shape, F32),
        scratch_shapes=[
            pltpu.VMEM((tokens, heads * hd), BF16),
            pltpu.VMEM((chunks, tokens, width // chunks), F32),
        ],
        compiler_params=pltpu.CompilerParams(vmem_limit_bytes=VMEM_LIMIT),
        cost_estimate=pl.CostEstimate(
            flops=2 * tokens * width * heads * hd,
            bytes_accessed=2 * width * heads * hd,
            transcendentals=tokens,
        ),
        name="output_stage",
    )(attended, w_out, x, w_lat, shifts, w_fin, step_size, added)


def prefix_of(place, everyone_ref):
    prefix = jnp.zeros(everyone_ref.shape[1:], F32)
    for step in range(everyone_ref.shape[0]):
        prefix += jnp.where(step < place, everyone_ref[step], 0.0)
    return prefix


def scan_kernel(place_ref, everyone_ref, start_ref, x_ref):
    place = place_ref[2]
    current = jnp.where(place == 0, start_ref[...], prefix_of(place, everyone_ref))
    x_ref[...] = jnp.broadcast_to(current.astype(BF16)[None], x_ref.shape)


def scan(place, everyone, start, chips):
    return pl.pallas_call(
        scan_kernel,
        in_specs=[pl.BlockSpec(memory_space=pltpu.SMEM)]
        + [pl.BlockSpec(memory_space=pltpu.VMEM)] * 2,
        out_shape=jax.ShapeDtypeStruct((chips,) + start.shape, BF16),
        compiler_params=pltpu.CompilerParams(vmem_limit_bytes=8 * MIB),
        name="scan",
    )(place, everyone, start)


def total_kernel(place_ref, everyone_ref, out_ref):
    place = place_ref[2]
    images, chans = out_ref.shape[0], out_ref.shape[2]
    pairs = everyone_ref.shape[1]
    for image in range(images):
        total = jnp.zeros(everyone_ref.shape[1:], F32)
        for step in range(everyone_ref.shape[0] // images):
            part = everyone_ref[step * images + image]
            total += jnp.where(step <= place, part, 0.0)
        out_ref[image, pl.ds(0, pairs, stride=2), :] = total[:, :chans]
        out_ref[image, pl.ds(1, pairs, stride=2), :] = total[:, chans:]


def total_rows(place, everyone, images, rows, chans):
    return pl.pallas_call(
        total_kernel,
        in_specs=[
            pl.BlockSpec(memory_space=pltpu.SMEM),
            pl.BlockSpec(memory_space=pltpu.VMEM),
        ],
        out_shape=jax.ShapeDtypeStruct((images, rows, chans), F32),
        compiler_params=pltpu.CompilerParams(vmem_limit_bytes=8 * MIB),
        name="total_rows",
    )(place, everyone)


def local(
    trajectory,
    noise,
    step_sizes,
    modulation,
    text_states,
    w_latent,
    w_image_qkv,
    w_text_kv,
    w_out_t,
    qk_gains,
    w_final,
):
    steps = lax.axis_size("step")
    chips = lax.axis_size(CHIPS)
    place, core = lax.axis_index("step"), lax.axis_index("core")
    seq = lax.axis_index(SEQ)
    images, rows, chans = trajectory.shape[1:]
    width = w_latent.shape[1]
    part, heads, hd = w_out_t.shape
    text_rows = text_states.shape[1] // steps
    shifts = modulation[0]

    mods = shifts[None, 3:5]
    back = shift_steps(mods, 1, steps)
    near = jnp.concatenate([mods, back])
    back = shift_steps(near, 2, steps)
    ahead = shift_steps(near, -2, steps)
    across = shift_steps(near, 4, steps)
    mods = jnp.concatenate([near, back, across, ahead])

    text_mine = lax.dynamic_slice_in_dim(text_states, place * text_rows, text_rows, 1)
    text_norm = layer_norm(text_mine.astype(F32)).astype(BF16)
    text_block = jnp.broadcast_to(
        text_norm.reshape(1, images, text_rows * width // hd, hd),
        (chips, images, text_rows * width // hd, hd),
    ).reshape(chips * images, -1, hd)
    weight_block = jnp.transpose(w_text_kv, (2, 1, 0, 3)).reshape(2 * heads, part, hd)
    start_pairs = trajectory[0].reshape(images, rows // 2, 2 * chans)
    latent_block = jnp.broadcast_to(
        start_pairs.astype(BF16)[None], (chips, images, rows // 2, 2 * chans)
    ).reshape(chips * images, rows // 2, 2 * chans)
    packed = jnp.concatenate([weight_block, text_block, latent_block], axis=1)
    columns = jnp.swapaxes(w_image_qkv.reshape(part, 3 * heads, hd), 0, 1)
    packed, w_latent, shifts, columns, w_out_t = lax.optimization_barrier(
        (packed, w_latent, shifts, columns, w_out_t)
    )
    w_out = lax.all_gather(w_out_t.reshape(part, heads * hd), SEQ, tiled=True)
    packed = lax.all_to_all(packed, SEQ, 0, 0, tiled=True)

    where = jnp.stack([seq, core, place]).astype(jnp.int32)
    keep, send, gram = fold(where, shifts, w_latent, columns, heads)
    mine = add_parts(keep, swap_cores(send))

    mine, packed, mods = lax.optimization_barrier((mine, packed, mods))
    mine = lax.all_to_all(mine, CHIPS, 0, 0, tiled=True)

    text_pairs = text_pairs_of(
        where, packed, swap_cores(packed), mods, qk_gains, text_rows * lax.axis_size(SEQ)
    )
    latents = packed[:, part + text_rows * width // hd :].reshape(-1, 2 * chans)

    received = [shift_steps(text_pairs[k], -k, steps) for k in (0, 1, 7, 2, 6, 3, 5, 4)]
    mine, received[:4], noise, start_pairs, w_final = lax.optimization_barrier(
        (mine, received[:4], noise, start_pairs, w_final)
    )
    text_pairs = jnp.concatenate(received, axis=0)
    mine = sum_parts(mine)
    theirs = swap_cores(mine)

    noise_pairs = noise[0].reshape(images, rows // 2, 2 * chans)
    own = jnp.concatenate(
        own_half(jnp.stack([noise_pairs, start_pairs], axis=1), core), axis=1
    )
    own_noise, own_start = own[0], own[1]
    added = own_noise + jnp.where(place == 0, own_start, jnp.zeros_like(own_start))
    w_fin = jnp.swapaxes(w_final, 0, 1)

    x_own = own_start.astype(BF16)
    for iteration in range(ITERS):
        attended = attention(where, latents, mine, theirs, gram, qk_gains, text_pairs, chips)
        attended = lax.all_to_all(attended, CHIPS, 0, 0, tiled=True)
        contrib = output_stage(
            attended, w_out, x_own, w_latent, shifts, w_fin, step_sizes, added, steps
        )
        if iteration + 1 < ITERS:
            everyone = lax.all_to_all(contrib, "step", 0, 0, tiled=True)
            latents = scan(where, everyone, own_start, chips)
            x_own = latents[0]
            latents = lax.all_to_all(latents, CHIPS, 0, 0, tiled=True).reshape(-1, 2 * chans)
    contrib = contrib.reshape(steps * images, rows // 2, 2 * chans)
    everyone = lax.all_to_all(contrib, ("step", "core"), 0, 0, tiled=True)
    return total_rows(where, everyone, images, rows, chans)[None]


def solution(mesh):
    steps = mesh.devices.shape[0]
    fine = Mesh(mesh.devices.reshape(steps, 4, 4, 2), ("step", "y", "x", "core"))
    placed = (
        P("step", None, SEQ, None),
        P("step", None, SEQ, None),
        P("step"),
        P("step", None, None),
        P(None, SEQ, None),
        P(),
        P(SEQ, None, None, None),
        P(SEQ, None, None, None),
        P(SEQ, None, None),
        P(),
        P(),
    )
    return jax.shard_map(
        local,
        mesh=fine,
        in_specs=placed,
        out_specs=P("step", None, SEQ, None),
        check_vma=False,
    )
```

```python
import math

import jax
import jax.numpy as jnp
from jax import lax
from jax.experimental import pallas as pl
from jax.experimental.pallas import tpu as pltpu
from jax.sharding import Mesh
from jax.sharding import PartitionSpec as P

ITERS = 2
CHIPS = ("y", "x")
SEQ = ("y", "x", "core")
F32, BF16 = jnp.float32, jnp.bfloat16
NT = (((1,), (1,)), ((), ()))
MIB = 1 << 20
LANES = 128
VMEM_LIMIT = 28 * MIB
FREE = pl.CostEstimate(flops=0, bytes_accessed=0, transcendentals=0)


def layer_norm(values):
    centre = values - jnp.mean(values, axis=-1, keepdims=True)
    spread = jnp.mean(centre * centre, axis=-1, keepdims=True)
    return centre * lax.rsqrt(spread + 1e-06)


def rms_scale(values, gains):
    return values * lax.rsqrt(jnp.mean(values * values, axis=-1, keepdims=True) + 1e-06) * gains


def swap_cores(values):
    return lax.ppermute(values, "core", [(0, 1), (1, 0)])


def own_half(values, core):
    kept = lax.dynamic_index_in_dim(values, core, 0, keepdims=False)
    came = swap_cores(lax.dynamic_index_in_dim(values, 1 - core, 0, keepdims=False))
    return jnp.where(core == 0, kept, came), jnp.where(core == 0, came, kept)


def shift_steps(values, by, steps):
    if by % steps == 0:
        return values
    return lax.ppermute(values, "step", [(i, (i + by) % steps) for i in range(steps)])


def fold_kernel(
    place_ref, shifts_ref, w_lat_ref, columns_ref, keep_ref, send_ref, gram_ref
):
    seq, core = place_ref[0], place_ref[1]
    chans, width = w_lat_ref.shape
    heads, sent = keep_ref.shape[:2]
    part, hd = columns_ref.shape[1:]
    half = chans // 2
    w_lat = w_lat_ref[...].astype(F32)
    mean = jnp.mean(w_lat, axis=1, keepdims=True)
    centred = w_lat - mean
    gram_ref[...] = (
        lax.dot_general(
            centred, centred, NT, precision=lax.Precision.HIGHEST, preferred_element_type=F32
        )
        / width
    )
    span = 2 * LANES
    first = seq * part
    base = jnp.minimum(first // LANES, (width - span) // LANES) * LANES
    window = pl.ds(pl.multiple_of(base, LANES), span)
    w_window = w_lat_ref[:, window].astype(F32) - mean
    left = jnp.concatenate(
        [
            w_window * (1.0 + shifts_ref[1:2, window]),
            shifts_ref[0:1, window],
            jnp.zeros((7, span), F32),
        ],
        axis=0,
    )
    left = pltpu.roll(left, lax.rem(span - (first - base), span), 1)[:, :part]
    count = left.shape[0]
    high = left.astype(BF16)
    low = (left - high.astype(F32)).astype(BF16)
    stacked = jnp.concatenate([high, low], axis=0)
    for head in range(heads):
        biases = []
        for kind in range(3):
            both = jnp.dot(
                stacked, columns_ref[kind * heads + head], preferred_element_type=F32
            )
            both = both[:count] + both[count:]
            rows = slice(kind * half, (kind + 1) * half)
            top, bottom = both[:half], both[half:chans]
            keep_ref[head, rows] = jnp.where(core == 0, top, bottom)
            send_ref[head, rows] = jnp.where(core == 0, bottom, top)
            biases.append(both[chans : chans + 1])
        biases.append(jnp.zeros((sent - 3 * half - 3, hd), F32))
        biases = jnp.concatenate(biases, axis=0)
        keep_ref[head, 3 * half :] = jnp.where(core == 0, biases, 0.0)
        send_ref[head, 3 * half :] = jnp.where(core == 0, 0.0, biases)


def fold(place, shifts, w_latent, columns, heads):
    chans = w_latent.shape[0]
    hd = columns.shape[2]
    sent = jax.ShapeDtypeStruct((heads, 3 * chans // 2 + 16, hd), F32)
    return pl.pallas_call(
        fold_kernel,
        in_specs=[pl.BlockSpec(memory_space=pltpu.SMEM)]
        + [pl.BlockSpec(memory_space=pltpu.VMEM)] * 3,
        out_shape=(sent, sent, jax.ShapeDtypeStruct((chans, chans), F32)),
        compiler_params=pltpu.CompilerParams(vmem_limit_bytes=24 * MIB),
        cost_estimate=FREE,
        name="fold",
    )(place, shifts, w_latent, columns)


def add_kernel(one_ref, other_ref, x_ref, out_ref):
    count = one_ref.shape[1]
    out_ref[:, :count] = (one_ref[...] + other_ref[...]).astype(BF16)
    for chip in range(out_ref.shape[0]):
        out_ref[chip, count:] = x_ref[...].astype(BF16)


def add_parts(one, other, x):
    chips, count, hd = one.shape
    return pl.pallas_call(
        add_kernel,
        out_shape=jax.ShapeDtypeStruct((chips, count + x.shape[0], hd), BF16),
        compiler_params=pltpu.CompilerParams(vmem_limit_bytes=8 * MIB),
        cost_estimate=FREE,
        name="add_parts",
    )(one, other, x)


def sum_kernel(parts_ref, out_ref, x_ref):
    count = out_ref.shape[0]
    total = parts_ref[0, :count].astype(F32)
    for part in range(1, parts_ref.shape[0]):
        total += parts_ref[part, :count].astype(F32)
    out_ref[...] = total
    x_ref[...] = parts_ref[:, count:]


def sum_parts(parts, below):
    chips, count, hd = parts.shape
    return pl.pallas_call(
        sum_kernel,
        out_shape=(
            jax.ShapeDtypeStruct((count - below, hd), F32),
            jax.ShapeDtypeStruct((chips, below, hd), BF16),
        ),
        compiler_params=pltpu.CompilerParams(vmem_limit_bytes=8 * MIB),
        cost_estimate=FREE,
        name="sum_parts",
    )(parts)


def text_kernel(
    place_ref, mine_ref, other_ref, mods_ref, gains_ref, out_ref, rows_ref, in_ref
):
    core = place_ref[1]
    sources = mine_ref.shape[0]
    steps, _, width = mods_ref.shape
    hd = gains_ref.shape[1]
    part = width // sources
    chunks = width // hd
    tokens = out_ref.shape[1]
    per = tokens // sources
    rows_ref[...] = mine_ref[:, part : part + per * chunks].astype(F32)
    for chunk in range(chunks):
        cut = slice(chunk * hd, (chunk + 1) * hd)
        text = jnp.concatenate(
            [rows_ref[:, row * chunks + chunk, :] for row in range(per)], axis=0
        )
        for step in range(steps):
            scale = 1.0 + mods_ref[step, 1:2, cut]
            in_ref[step * tokens : (step + 1) * tokens, cut] = (
                text * scale + mods_ref[step, 0:1, cut]
            ).astype(BF16)
    text_in = in_ref[...]
    mine = jnp.dot(
        text_in, mine_ref[:, :part].reshape(width, hd), preferred_element_type=F32
    )
    other = jnp.dot(
        text_in, other_ref[:, :part].reshape(width, hd), preferred_element_type=F32
    )
    keys = rms_scale(jnp.where(core == 0, mine, other), gains_ref[2:3]).astype(BF16)
    values = jnp.where(core == 0, other, mine).astype(BF16)
    out_ref[:, :, :hd] = keys.reshape(steps, tokens, hd)
    out_ref[:, :, hd:] = values.reshape(steps, tokens, hd)


def text_pairs_of(place, mine, other, mods, gains, tokens):
    steps, _, width = mods.shape
    sources, _, hd = mine.shape
    return pl.pallas_call(
        text_kernel,
        in_specs=[pl.BlockSpec(memory_space=pltpu.SMEM)]
        + [pl.BlockSpec(memory_space=pltpu.VMEM)] * 4,
        out_shape=jax.ShapeDtypeStruct((steps, tokens, 2 * hd), BF16),
        scratch_shapes=[
            pltpu.VMEM((sources, tokens // sources * (width // hd), hd), F32),
            pltpu.VMEM((steps * tokens, width), BF16),
        ],
        compiler_params=pltpu.CompilerParams(vmem_limit_bytes=24 * MIB),
        cost_estimate=FREE,
        name="text_pairs",
    )(place, mine, other, mods, gains)


def attention_kernel(
    place_ref, x_ref, mine_ref, theirs_ref, gram_ref, gains_ref, text_ref, out_ref,
    q_ref, k_ref, v_ref
):
    core = place_ref[1]
    hd = gains_ref.shape[1]
    chans = gram_ref.shape[0]
    half_chans = chans // 2
    pairs = x_ref.shape[0]
    text = text_ref.shape[0]
    chips, block, _ = out_ref.shape
    factor = math.log2(math.e) / math.sqrt(hd)
    x = x_ref[...]
    doubled = jnp.concatenate([x, x], axis=1)
    first = jnp.where(core == 0, mine_ref[...], theirs_ref[...])
    second = jnp.where(core == 0, theirs_ref[...], mine_ref[...])
    folded = []
    for kind in range(3):
        rows = slice(kind * half_chans, (kind + 1) * half_chans)
        folded.append(jnp.concatenate([first[rows], second[rows]], axis=0))
    bias = [first[3 * half_chans + kind : 3 * half_chans + kind + 1] for kind in range(3)]
    blank = jnp.zeros((chans, 4 * hd), BF16)
    k_ref[:text] = text_ref[:, :hd]
    v_ref[:text, :hd] = text_ref[:, hd:]
    v_ref[:, hd:] = jnp.ones((v_ref.shape[0], hd), BF16)
    none = jnp.zeros((chans, chans), F32)
    for parity in range(2):
        grams = [gram_ref[...], none] if parity == 0 else [none, gram_ref[...]]
        weights = jnp.concatenate(folded + grams, axis=1)
        high = weights.astype(BF16)
        low = (weights - high.astype(F32)).astype(BF16)
        rows = [high, blank, low, blank] if parity == 0 else [blank, high, blank, low]
        projected = jnp.dot(
            doubled, jnp.concatenate(rows, axis=0), preferred_element_type=F32
        )
        spread = jnp.sum(projected[:, 3 * hd :] * x.astype(F32), axis=1, keepdims=True)
        scale = lax.rsqrt(spread + 1e-06)
        mine = pl.ds(parity * pairs, pairs)
        image = pl.ds(text + parity * pairs, pairs)
        queries = projected[:, :hd] * scale + bias[0]
        image_keys = projected[:, hd : 2 * hd] * scale + bias[1]
        q_ref[mine] = rms_scale(queries, gains_ref[0:1]).astype(BF16)
        k_ref[image] = rms_scale(image_keys, gains_ref[1:2]).astype(BF16)
        v_ref[image, :hd] = (projected[:, 2 * hd : 3 * hd] * scale + bias[2]).astype(BF16)
    half = block // 2
    size = 128
    for start in range(0, 2 * pairs, size):
        scores = lax.dot_general(
            q_ref[start : start + size], k_ref[...], NT, preferred_element_type=F32
        )
        powers = jnp.exp2(scores * factor).astype(BF16)
        both = jnp.dot(powers, v_ref[...], preferred_element_type=F32)
        attended = (both[:, :hd] / both[:, hd:]).astype(BF16)
        parity, begin = divmod(start, pairs)
        out_ref[begin // half : (begin + size) // half, parity * half : (parity + 1) * half] = (
            attended.reshape(size // half, half, hd)
        )


def attention(place, latents, mine, theirs, gram, gains, text_pairs, chips):
    pairs = latents.shape[0]
    text, hd = text_pairs.shape[0], gains.shape[1]
    keys = text + 2 * pairs
    return pl.pallas_call(
        attention_kernel,
        in_specs=[pl.BlockSpec(memory_space=pltpu.SMEM)]
        + [pl.BlockSpec(memory_space=pltpu.VMEM)] * 6,
        out_shape=jax.ShapeDtypeStruct((chips, 2 * pairs // chips, hd), BF16),
        scratch_shapes=[
            pltpu.VMEM((2 * pairs, hd), BF16),
            pltpu.VMEM((keys, hd), BF16),
            pltpu.VMEM((keys, 2 * hd), BF16),
        ],
        compiler_params=pltpu.CompilerParams(vmem_limit_bytes=VMEM_LIMIT),
        cost_estimate=pl.CostEstimate(
            flops=8 * pairs * keys * hd, bytes_accessed=2 * MIB, transcendentals=2 * pairs * keys
        ),
        name="attention",
    )(place, latents, mine, theirs, gram, gains, text_pairs)


def output_kernel(
    attended_ref, w_out_ref, x_ref, w_lat_ref, shifts_ref, w_fin_ref, step_ref, added_ref,
    out_ref, rows_ref, mixed_ref
):
    heads, tokens, hd = attended_ref.shape
    chunks = mixed_ref.shape[0]
    chans, width = w_lat_ref.shape
    size = width // chunks
    half = tokens // 2
    for head in range(heads):
        rows_ref[:, head * hd : (head + 1) * hd] = attended_ref[head]
    x = x_ref[...].astype(F32)
    x = jnp.concatenate([x[:, :chans], x[:, chans:]], axis=0).astype(BF16)
    total = jnp.zeros((tokens, 1), F32)
    for c in range(chunks):
        cut = slice(c * size, (c + 1) * size)
        mixed = lax.dot_general(rows_ref[...], w_out_ref[cut], NT, preferred_element_type=F32)
        hidden = jnp.dot(x, w_lat_ref[:, cut], preferred_element_type=F32)
        combined = hidden + shifts_ref[2:3, cut] * mixed
        mixed_ref[c] = combined
        total += jnp.sum(combined, axis=1, keepdims=True)
    mean = total / width
    total = jnp.zeros((tokens, 1), F32)
    for c in range(chunks):
        centre = mixed_ref[c] - mean
        total += jnp.sum(centre * centre, axis=1, keepdims=True)
    scale = lax.rsqrt(total / width + 1e-06)
    drift = jnp.zeros((tokens, chans), F32)
    for c in range(chunks):
        cut = slice(c * size, (c + 1) * size)
        normal = (mixed_ref[c] - mean) * scale
        final_in = (normal * (1.0 + shifts_ref[6:7, cut]) + shifts_ref[5:6, cut]).astype(BF16)
        drift += lax.dot_general(final_in, w_fin_ref[:, cut], NT, preferred_element_type=F32)
    drift = jnp.concatenate([drift[:half], drift[half:]], axis=1)
    contrib = step_ref[0] * drift + added_ref[...]
    out_ref[...] = jnp.broadcast_to(contrib[None], out_ref.shape)


def output_stage(attended, w_out, x, w_lat, shifts, w_fin, step_size, added, steps):
    heads, tokens, hd = attended.shape
    width = w_out.shape[0]
    chunks = 12
    vmem = pl.BlockSpec(memory_space=pltpu.VMEM)
    return pl.pallas_call(
        output_kernel,
        in_specs=[
            vmem,
            vmem,
            vmem,
            vmem,
            vmem,
            vmem,
            pl.BlockSpec(memory_space=pltpu.SMEM),
            vmem,
        ],
        out_shape=jax.ShapeDtypeStruct((steps,) + added.shape, F32),
        scratch_shapes=[
            pltpu.VMEM((tokens, heads * hd), BF16),
            pltpu.VMEM((chunks, tokens, width // chunks), F32),
        ],
        compiler_params=pltpu.CompilerParams(vmem_limit_bytes=VMEM_LIMIT),
        cost_estimate=pl.CostEstimate(
            flops=2 * tokens * width * heads * hd,
            bytes_accessed=2 * width * heads * hd,
            transcendentals=tokens,
        ),
        name="output_stage",
    )(attended, w_out, x, w_lat, shifts, w_fin, step_size, added)


def prefix_of(place, everyone_ref):
    prefix = jnp.zeros(everyone_ref.shape[1:], F32)
    for step in range(everyone_ref.shape[0]):
        prefix += jnp.where(step < place, everyone_ref[step], 0.0)
    return prefix


def scan_kernel(place_ref, everyone_ref, start_ref, x_ref):
    place = place_ref[2]
    current = jnp.where(place == 0, start_ref[...], prefix_of(place, everyone_ref))
    x_ref[...] = jnp.broadcast_to(current.astype(BF16)[None], x_ref.shape)


def scan(place, everyone, start, chips):
    return pl.pallas_call(
        scan_kernel,
        in_specs=[pl.BlockSpec(memory_space=pltpu.SMEM)]
        + [pl.BlockSpec(memory_space=pltpu.VMEM)] * 2,
        out_shape=jax.ShapeDtypeStruct((chips,) + start.shape, BF16),
        compiler_params=pltpu.CompilerParams(vmem_limit_bytes=8 * MIB),
        name="scan",
    )(place, everyone, start)


def total_kernel(place_ref, everyone_ref, out_ref):
    place = place_ref[2]
    images, chans = out_ref.shape[0], out_ref.shape[2]
    pairs = everyone_ref.shape[1]
    for image in range(images):
        total = jnp.zeros(everyone_ref.shape[1:], F32)
        for step in range(everyone_ref.shape[0] // images):
            part = everyone_ref[step * images + image]
            total += jnp.where(step <= place, part, 0.0)
        out_ref[image, pl.ds(0, pairs, stride=2), :] = total[:, :chans]
        out_ref[image, pl.ds(1, pairs, stride=2), :] = total[:, chans:]


def total_rows(place, everyone, images, rows, chans):
    return pl.pallas_call(
        total_kernel,
        in_specs=[
            pl.BlockSpec(memory_space=pltpu.SMEM),
            pl.BlockSpec(memory_space=pltpu.VMEM),
        ],
        out_shape=jax.ShapeDtypeStruct((images, rows, chans), F32),
        compiler_params=pltpu.CompilerParams(vmem_limit_bytes=8 * MIB),
        name="total_rows",
    )(place, everyone)


def local(
    trajectory,
    noise,
    step_sizes,
    modulation,
    text_states,
    w_latent,
    w_image_qkv,
    w_text_kv,
    w_out_t,
    qk_gains,
    w_final,
):
    steps = lax.axis_size("step")
    chips = lax.axis_size(CHIPS)
    place, core = lax.axis_index("step"), lax.axis_index("core")
    seq = lax.axis_index(SEQ)
    images, rows, chans = trajectory.shape[1:]
    width = w_latent.shape[1]
    part, heads, hd = w_out_t.shape
    text_rows = text_states.shape[1] // steps
    shifts = modulation[0]

    mods = shifts[None, 3:5]
    back = shift_steps(mods, 1, steps)
    near = jnp.concatenate([mods, back])
    back = shift_steps(near, 2, steps)
    ahead = shift_steps(near, -2, steps)
    across = shift_steps(near, 4, steps)
    mods = jnp.concatenate([near, back, across, ahead])

    text_mine = lax.dynamic_slice_in_dim(text_states, place * text_rows, text_rows, 1)
    text_norm = layer_norm(text_mine.astype(F32)).astype(BF16)
    text_block = jnp.broadcast_to(
        text_norm.reshape(1, images, text_rows * width // hd, hd),
        (chips, images, text_rows * width // hd, hd),
    ).reshape(chips * images, -1, hd)
    weight_block = jnp.transpose(w_text_kv, (2, 1, 0, 3)).reshape(2 * heads, part, hd)
    start_pairs = trajectory[0].reshape(images, rows // 2, 2 * chans)
    packed = jnp.concatenate([weight_block, text_block], axis=1)
    columns = jnp.swapaxes(w_image_qkv.reshape(part, 3 * heads, hd), 0, 1)
    packed, w_latent, shifts, columns, w_out_t = lax.optimization_barrier(
        (packed, w_latent, shifts, columns, w_out_t)
    )
    w_out = lax.all_gather(w_out_t.reshape(part, heads * hd), SEQ, tiled=True)
    packed = lax.all_to_all(packed, SEQ, 0, 0, tiled=True)

    where = jnp.stack([seq, core, place]).astype(jnp.int32)
    keep, send, gram = fold(where, shifts, w_latent, columns, heads)
    noise_pairs = noise[0].reshape(images, rows // 2, 2 * chans)
    own = jnp.concatenate(
        own_half(jnp.stack([noise_pairs, start_pairs], axis=1), core), axis=1
    )
    own_noise, own_start = own[0], own[1]
    mine = add_parts(keep, swap_cores(send), own_start)

    mine, packed, mods = lax.optimization_barrier((mine, packed, mods))
    mine = lax.all_to_all(mine, CHIPS, 0, 0, tiled=True)

    text_pairs = text_pairs_of(
        where, packed, swap_cores(packed), mods, qk_gains, text_rows * lax.axis_size(SEQ)
    )
    received = [shift_steps(text_pairs[k], -k, steps) for k in (0, 1, 7, 2, 6, 3, 5, 4)]
    mine, received[:4], w_final = lax.optimization_barrier((mine, received[:4], w_final))
    text_pairs = jnp.concatenate(received, axis=0)
    mine, latents = sum_parts(mine, rows)
    latents = latents.reshape(-1, 2 * chans)
    theirs = swap_cores(mine)

    added = own_noise + jnp.where(place == 0, own_start, jnp.zeros_like(own_start))
    w_fin = jnp.swapaxes(w_final, 0, 1)

    x_own = own_start.astype(BF16)
    for iteration in range(ITERS):
        attended = attention(where, latents, mine, theirs, gram, qk_gains, text_pairs, chips)
        attended = lax.all_to_all(attended, CHIPS, 0, 0, tiled=True)
        contrib = output_stage(
            attended, w_out, x_own, w_latent, shifts, w_fin, step_sizes, added, steps
        )
        if iteration + 1 < ITERS:
            everyone = lax.all_to_all(contrib, "step", 0, 0, tiled=True)
            latents = scan(where, everyone, own_start, chips)
            x_own = latents[0]
            latents = lax.all_to_all(latents, CHIPS, 0, 0, tiled=True).reshape(-1, 2 * chans)
    contrib = contrib.reshape(steps * images, rows // 2, 2 * chans)
    everyone = lax.all_to_all(contrib, ("step", "core"), 0, 0, tiled=True)
    return total_rows(where, everyone, images, rows, chans)[None]


def solution(mesh):
    steps = mesh.devices.shape[0]
    fine = Mesh(mesh.devices.reshape(steps, 4, 4, 2), ("step", "y", "x", "core"))
    placed = (
        P("step", None, SEQ, None),
        P("step", None, SEQ, None),
        P("step"),
        P("step", None, None),
        P(None, SEQ, None),
        P(),
        P(SEQ, None, None, None),
        P(SEQ, None, None, None),
        P(SEQ, None, None),
        P(),
        P(),
    )
    return jax.shard_map(
        local,
        mesh=fine,
        in_specs=placed,
        out_specs=P("step", None, SEQ, None),
        check_vma=False,
    )
```

```python
import math

import jax
import jax.numpy as jnp
from jax import lax
from jax.experimental import pallas as pl
from jax.experimental.pallas import tpu as pltpu
from jax.sharding import Mesh
from jax.sharding import PartitionSpec as P

ITERS = 2
CHIPS = ("y", "x")
SEQ = ("y", "x", "core")
F32, BF16 = jnp.float32, jnp.bfloat16
NT = (((1,), (1,)), ((), ()))
MIB = 1 << 20
LANES = 128
VMEM_LIMIT = 28 * MIB
FREE = pl.CostEstimate(flops=0, bytes_accessed=0, transcendentals=0)


def layer_norm(values):
    centre = values - jnp.mean(values, axis=-1, keepdims=True)
    spread = jnp.mean(centre * centre, axis=-1, keepdims=True)
    return centre * lax.rsqrt(spread + 1e-06)


def rms_scale(values, gains):
    return values * lax.rsqrt(jnp.mean(values * values, axis=-1, keepdims=True) + 1e-06) * gains


def swap_cores(values):
    return lax.ppermute(values, "core", [(0, 1), (1, 0)])


def own_half(values, core):
    kept = lax.dynamic_index_in_dim(values, core, 0, keepdims=False)
    came = swap_cores(lax.dynamic_index_in_dim(values, 1 - core, 0, keepdims=False))
    return jnp.where(core == 0, kept, came), jnp.where(core == 0, came, kept)


def shift_steps(values, by, steps):
    if by % steps == 0:
        return values
    return lax.ppermute(values, "step", [(i, (i + by) % steps) for i in range(steps)])


def fold_kernel(
    place_ref, shifts_ref, w_lat_ref, columns_ref, keep_ref, send_ref, gram_ref
):
    seq, core = place_ref[0], place_ref[1]
    chans, width = w_lat_ref.shape
    heads, sent = keep_ref.shape[:2]
    part, hd = columns_ref.shape[1:]
    half = chans // 2
    w_lat = w_lat_ref[...].astype(F32)
    mean = jnp.mean(w_lat, axis=1, keepdims=True)
    centred = w_lat - mean
    gram_ref[...] = (
        lax.dot_general(
            centred, centred, NT, precision=lax.Precision.HIGHEST, preferred_element_type=F32
        )
        / width
    )
    span = 2 * LANES
    first = seq * part
    base = jnp.minimum(first // LANES, (width - span) // LANES) * LANES
    window = pl.ds(pl.multiple_of(base, LANES), span)
    w_window = w_lat_ref[:, window].astype(F32) - mean
    left = jnp.concatenate(
        [
            w_window * (1.0 + shifts_ref[1:2, window]),
            shifts_ref[0:1, window],
            jnp.zeros((7, span), F32),
        ],
        axis=0,
    )
    left = pltpu.roll(left, lax.rem(span - (first - base), span), 1)[:, :part]
    count = left.shape[0]
    high = left.astype(BF16)
    low = (left - high.astype(F32)).astype(BF16)
    stacked = jnp.concatenate([high, low], axis=0)
    for head in range(heads):
        biases = []
        for kind in range(3):
            both = jnp.dot(
                stacked, columns_ref[kind * heads + head], preferred_element_type=F32
            )
            both = both[:count] + both[count:]
            rows = slice(kind * half, (kind + 1) * half)
            top, bottom = both[:half], both[half:chans]
            keep_ref[head, rows] = jnp.where(core == 0, top, bottom)
            send_ref[head, rows] = jnp.where(core == 0, bottom, top)
            biases.append(both[chans : chans + 1])
        biases.append(jnp.zeros((sent - 3 * half - 3, hd), F32))
        biases = jnp.concatenate(biases, axis=0)
        keep_ref[head, 3 * half :] = jnp.where(core == 0, biases, 0.0)
        send_ref[head, 3 * half :] = jnp.where(core == 0, 0.0, biases)


def fold(place, shifts, w_latent, columns, heads):
    chans = w_latent.shape[0]
    hd = columns.shape[2]
    sent = jax.ShapeDtypeStruct((heads, 3 * chans // 2 + 16, hd), F32)
    return pl.pallas_call(
        fold_kernel,
        in_specs=[pl.BlockSpec(memory_space=pltpu.SMEM)]
        + [pl.BlockSpec(memory_space=pltpu.VMEM)] * 3,
        out_shape=(sent, sent, jax.ShapeDtypeStruct((chans, chans), F32)),
        compiler_params=pltpu.CompilerParams(vmem_limit_bytes=16 * MIB),
        cost_estimate=FREE,
        name="fold",
    )(place, shifts, w_latent, columns)


def add_kernel(one_ref, other_ref, x_ref, out_ref):
    count = one_ref.shape[1]
    out_ref[:, :count] = (one_ref[...] + other_ref[...]).astype(BF16)
    for chip in range(out_ref.shape[0]):
        out_ref[chip, count:] = x_ref[...].astype(BF16)


def add_parts(one, other, x):
    chips, count, hd = one.shape
    return pl.pallas_call(
        add_kernel,
        out_shape=jax.ShapeDtypeStruct((chips, count + x.shape[0], hd), BF16),
        compiler_params=pltpu.CompilerParams(vmem_limit_bytes=8 * MIB),
        cost_estimate=FREE,
        name="add_parts",
    )(one, other, x)


def sum_kernel(parts_ref, out_ref, x_ref):
    count = out_ref.shape[0]
    total = parts_ref[0, :count].astype(F32)
    for part in range(1, parts_ref.shape[0]):
        total += parts_ref[part, :count].astype(F32)
    out_ref[...] = total
    x_ref[...] = parts_ref[:, count:]


def sum_parts(parts, below):
    chips, count, hd = parts.shape
    return pl.pallas_call(
        sum_kernel,
        out_shape=(
            jax.ShapeDtypeStruct((count - below, hd), F32),
            jax.ShapeDtypeStruct((chips, below, hd), BF16),
        ),
        compiler_params=pltpu.CompilerParams(vmem_limit_bytes=8 * MIB),
        cost_estimate=FREE,
        name="sum_parts",
    )(parts)


def text_kernel(
    place_ref, mine_ref, other_ref, mods_ref, gains_ref, out_ref, rows_ref, in_ref
):
    core = place_ref[1]
    sources = mine_ref.shape[0]
    steps, _, width = mods_ref.shape
    hd = gains_ref.shape[1]
    part = width // sources
    chunks = width // hd
    tokens = out_ref.shape[1]
    per = tokens // sources
    rows_ref[...] = mine_ref[:, part : part + per * chunks].astype(F32)
    for chunk in range(chunks):
        cut = slice(chunk * hd, (chunk + 1) * hd)
        text = jnp.concatenate(
            [rows_ref[:, row * chunks + chunk, :] for row in range(per)], axis=0
        )
        for step in range(steps):
            scale = 1.0 + mods_ref[step, 1:2, cut]
            in_ref[step * tokens : (step + 1) * tokens, cut] = (
                text * scale + mods_ref[step, 0:1, cut]
            ).astype(BF16)
    text_in = in_ref[...]
    mine = jnp.dot(
        text_in, mine_ref[:, :part].reshape(width, hd), preferred_element_type=F32
    )
    other = jnp.dot(
        text_in, other_ref[:, :part].reshape(width, hd), preferred_element_type=F32
    )
    keys = rms_scale(jnp.where(core == 0, mine, other), gains_ref[2:3]).astype(BF16)
    values = jnp.where(core == 0, other, mine).astype(BF16)
    out_ref[:, :, :hd] = keys.reshape(steps, tokens, hd)
    out_ref[:, :, hd:] = values.reshape(steps, tokens, hd)


def text_pairs_of(place, mine, other, mods, gains, tokens):
    steps, _, width = mods.shape
    sources, _, hd = mine.shape
    return pl.pallas_call(
        text_kernel,
        in_specs=[pl.BlockSpec(memory_space=pltpu.SMEM)]
        + [pl.BlockSpec(memory_space=pltpu.VMEM)] * 4,
        out_shape=jax.ShapeDtypeStruct((steps, tokens, 2 * hd), BF16),
        scratch_shapes=[
            pltpu.VMEM((sources, tokens // sources * (width // hd), hd), F32),
            pltpu.VMEM((steps * tokens, width), BF16),
        ],
        compiler_params=pltpu.CompilerParams(vmem_limit_bytes=16 * MIB),
        cost_estimate=FREE,
        name="text_pairs",
    )(place, mine, other, mods, gains)


def attention_kernel(
    place_ref, x_ref, mine_ref, theirs_ref, gram_ref, gains_ref, text_ref, out_ref,
    q_ref, k_ref, v_ref
):
    core = place_ref[1]
    hd = gains_ref.shape[1]
    chans = gram_ref.shape[0]
    half_chans = chans // 2
    pairs = x_ref.shape[0]
    text = text_ref.shape[0]
    chips, block, _ = out_ref.shape
    factor = math.log2(math.e) / math.sqrt(hd)
    x = x_ref[...]
    doubled = jnp.concatenate([x, x], axis=1)
    first = jnp.where(core == 0, mine_ref[...], theirs_ref[...])
    second = jnp.where(core == 0, theirs_ref[...], mine_ref[...])
    folded = []
    for kind in range(3):
        rows = slice(kind * half_chans, (kind + 1) * half_chans)
        folded.append(jnp.concatenate([first[rows], second[rows]], axis=0))
    bias = [first[3 * half_chans + kind : 3 * half_chans + kind + 1] for kind in range(3)]
    blank = jnp.zeros((chans, 4 * hd), BF16)
    k_ref[:text] = text_ref[:, :hd]
    v_ref[:text, :hd] = text_ref[:, hd:]
    v_ref[:, hd:] = jnp.ones((v_ref.shape[0], hd), BF16)
    none = jnp.zeros((chans, chans), F32)
    for parity in range(2):
        grams = [gram_ref[...], none] if parity == 0 else [none, gram_ref[...]]
        weights = jnp.concatenate(folded + grams, axis=1)
        high = weights.astype(BF16)
        low = (weights - high.astype(F32)).astype(BF16)
        rows = [high, blank, low, blank] if parity == 0 else [blank, high, blank, low]
        projected = jnp.dot(
            doubled, jnp.concatenate(rows, axis=0), preferred_element_type=F32
        )
        spread = jnp.sum(projected[:, 3 * hd :] * x.astype(F32), axis=1, keepdims=True)
        scale = lax.rsqrt(spread + 1e-06)
        mine = pl.ds(parity * pairs, pairs)
        image = pl.ds(text + parity * pairs, pairs)
        queries = projected[:, :hd] * scale + bias[0]
        image_keys = projected[:, hd : 2 * hd] * scale + bias[1]
        q_ref[mine] = rms_scale(queries, gains_ref[0:1]).astype(BF16)
        k_ref[image] = rms_scale(image_keys, gains_ref[1:2]).astype(BF16)
        v_ref[image, :hd] = (projected[:, 2 * hd : 3 * hd] * scale + bias[2]).astype(BF16)
    half = block // 2
    size = 128
    for start in range(0, 2 * pairs, size):
        scores = lax.dot_general(
            q_ref[start : start + size], k_ref[...], NT, preferred_element_type=F32
        )
        powers = jnp.exp2(scores * factor).astype(BF16)
        both = jnp.dot(powers, v_ref[...], preferred_element_type=F32)
        attended = (both[:, :hd] / both[:, hd:]).astype(BF16)
        parity, begin = divmod(start, pairs)
        out_ref[begin // half : (begin + size) // half, parity * half : (parity + 1) * half] = (
            attended.reshape(size // half, half, hd)
        )


def attention(place, latents, mine, theirs, gram, gains, text_pairs, chips):
    pairs = latents.shape[0]
    text, hd = text_pairs.shape[0], gains.shape[1]
    keys = text + 2 * pairs
    return pl.pallas_call(
        attention_kernel,
        in_specs=[pl.BlockSpec(memory_space=pltpu.SMEM)]
        + [pl.BlockSpec(memory_space=pltpu.VMEM)] * 6,
        out_shape=jax.ShapeDtypeStruct((chips, 2 * pairs // chips, hd), BF16),
        scratch_shapes=[
            pltpu.VMEM((2 * pairs, hd), BF16),
            pltpu.VMEM((keys, hd), BF16),
            pltpu.VMEM((keys, 2 * hd), BF16),
        ],
        compiler_params=pltpu.CompilerParams(vmem_limit_bytes=VMEM_LIMIT),
        cost_estimate=pl.CostEstimate(
            flops=8 * pairs * keys * hd, bytes_accessed=2 * MIB, transcendentals=2 * pairs * keys
        ),
        name="attention",
    )(place, latents, mine, theirs, gram, gains, text_pairs)


def output_kernel(
    attended_ref, w_out_ref, x_ref, w_lat_ref, shifts_ref, w_fin_ref, step_ref, added_ref,
    out_ref, rows_ref, mixed_ref
):
    heads, tokens, hd = attended_ref.shape
    chunks = mixed_ref.shape[0]
    chans, width = w_lat_ref.shape
    size = width // chunks
    half = tokens // 2
    for head in range(heads):
        rows_ref[:, head * hd : (head + 1) * hd] = attended_ref[head]
    x = x_ref[...].astype(F32)
    x = jnp.concatenate([x[:, :chans], x[:, chans:]], axis=0).astype(BF16)
    total = jnp.zeros((tokens, 1), F32)
    for c in range(chunks):
        cut = slice(c * size, (c + 1) * size)
        mixed = lax.dot_general(rows_ref[...], w_out_ref[cut], NT, preferred_element_type=F32)
        hidden = jnp.dot(x, w_lat_ref[:, cut], preferred_element_type=F32)
        combined = hidden + shifts_ref[2:3, cut] * mixed
        mixed_ref[c] = combined
        total += jnp.sum(combined, axis=1, keepdims=True)
    mean = total / width
    total = jnp.zeros((tokens, 1), F32)
    for c in range(chunks):
        centre = mixed_ref[c] - mean
        total += jnp.sum(centre * centre, axis=1, keepdims=True)
    scale = lax.rsqrt(total / width + 1e-06)
    drift = jnp.zeros((tokens, chans), F32)
    for c in range(chunks):
        cut = slice(c * size, (c + 1) * size)
        normal = (mixed_ref[c] - mean) * scale
        final_in = (normal * (1.0 + shifts_ref[6:7, cut]) + shifts_ref[5:6, cut]).astype(BF16)
        drift += lax.dot_general(final_in, w_fin_ref[:, cut], NT, preferred_element_type=F32)
    drift = jnp.concatenate([drift[:half], drift[half:]], axis=1)
    contrib = step_ref[0] * drift + added_ref[...]
    out_ref[...] = jnp.broadcast_to(contrib[None], out_ref.shape)


def output_stage(attended, w_out, x, w_lat, shifts, w_fin, step_size, added, steps):
    heads, tokens, hd = attended.shape
    width = w_out.shape[0]
    chunks = 12
    vmem = pl.BlockSpec(memory_space=pltpu.VMEM)
    return pl.pallas_call(
        output_kernel,
        in_specs=[
            vmem,
            vmem,
            vmem,
            vmem,
            vmem,
            vmem,
            pl.BlockSpec(memory_space=pltpu.SMEM),
            vmem,
        ],
        out_shape=jax.ShapeDtypeStruct((steps,) + added.shape, F32),
        scratch_shapes=[
            pltpu.VMEM((tokens, heads * hd), BF16),
            pltpu.VMEM((chunks, tokens, width // chunks), F32),
        ],
        compiler_params=pltpu.CompilerParams(vmem_limit_bytes=VMEM_LIMIT),
        cost_estimate=pl.CostEstimate(
            flops=2 * tokens * width * heads * hd,
            bytes_accessed=2 * width * heads * hd,
            transcendentals=tokens,
        ),
        name="output_stage",
    )(attended, w_out, x, w_lat, shifts, w_fin, step_size, added)


def prefix_of(place, everyone_ref):
    prefix = jnp.zeros(everyone_ref.shape[1:], F32)
    for step in range(everyone_ref.shape[0]):
        prefix += jnp.where(step < place, everyone_ref[step], 0.0)
    return prefix


def scan_kernel(place_ref, everyone_ref, start_ref, x_ref):
    place = place_ref[2]
    current = jnp.where(place == 0, start_ref[...], prefix_of(place, everyone_ref))
    x_ref[...] = jnp.broadcast_to(current.astype(BF16)[None], x_ref.shape)


def scan(place, everyone, start, chips):
    return pl.pallas_call(
        scan_kernel,
        in_specs=[pl.BlockSpec(memory_space=pltpu.SMEM)]
        + [pl.BlockSpec(memory_space=pltpu.VMEM)] * 2,
        out_shape=jax.ShapeDtypeStruct((chips,) + start.shape, BF16),
        compiler_params=pltpu.CompilerParams(vmem_limit_bytes=8 * MIB),
        name="scan",
    )(place, everyone, start)


def total_kernel(place_ref, everyone_ref, out_ref):
    place = place_ref[2]
    images, chans = out_ref.shape[0], out_ref.shape[2]
    pairs = everyone_ref.shape[1]
    for image in range(images):
        total = jnp.zeros(everyone_ref.shape[1:], F32)
        for step in range(everyone_ref.shape[0] // images):
            part = everyone_ref[step * images + image]
            total += jnp.where(step <= place, part, 0.0)
        out_ref[image, pl.ds(0, pairs, stride=2), :] = total[:, :chans]
        out_ref[image, pl.ds(1, pairs, stride=2), :] = total[:, chans:]


def total_rows(place, everyone, images, rows, chans):
    return pl.pallas_call(
        total_kernel,
        in_specs=[
            pl.BlockSpec(memory_space=pltpu.SMEM),
            pl.BlockSpec(memory_space=pltpu.VMEM),
        ],
        out_shape=jax.ShapeDtypeStruct((images, rows, chans), F32),
        compiler_params=pltpu.CompilerParams(vmem_limit_bytes=8 * MIB),
        name="total_rows",
    )(place, everyone)


def local(
    trajectory,
    noise,
    step_sizes,
    modulation,
    text_states,
    w_latent,
    w_image_qkv,
    w_text_kv,
    w_out_t,
    qk_gains,
    w_final,
):
    steps = lax.axis_size("step")
    chips = lax.axis_size(CHIPS)
    place, core = lax.axis_index("step"), lax.axis_index("core")
    seq = lax.axis_index(SEQ)
    images, rows, chans = trajectory.shape[1:]
    width = w_latent.shape[1]
    part, heads, hd = w_out_t.shape
    text_rows = text_states.shape[1] // steps
    shifts = modulation[0]

    mods = shifts[None, 3:5]
    back = shift_steps(mods, 1, steps)
    near = jnp.concatenate([mods, back])
    back = shift_steps(near, 2, steps)
    ahead = shift_steps(near, -2, steps)
    across = shift_steps(near, 4, steps)
    mods = jnp.concatenate([near, back, across, ahead])

    text_mine = lax.dynamic_slice_in_dim(text_states, place * text_rows, text_rows, 1)
    text_norm = layer_norm(text_mine.astype(F32)).astype(BF16)
    text_block = jnp.broadcast_to(
        text_norm.reshape(1, images, text_rows * width // hd, hd),
        (chips, images, text_rows * width // hd, hd),
    ).reshape(chips * images, -1, hd)
    weight_block = jnp.transpose(w_text_kv, (2, 1, 0, 3)).reshape(2 * heads, part, hd)
    start_pairs = trajectory[0].reshape(images, rows // 2, 2 * chans)
    packed = jnp.concatenate([weight_block, text_block], axis=1)
    columns = jnp.swapaxes(w_image_qkv.reshape(part, 3 * heads, hd), 0, 1)
    packed, w_latent, shifts, columns, w_out_t = lax.optimization_barrier(
        (packed, w_latent, shifts, columns, w_out_t)
    )
    w_out = lax.all_gather(w_out_t.reshape(part, heads * hd), SEQ, tiled=True)
    packed = lax.all_to_all(packed, SEQ, 0, 0, tiled=True)

    where = jnp.stack([seq, core, place]).astype(jnp.int32)
    keep, send, gram = fold(where, shifts, w_latent, columns, heads)
    noise_pairs = noise[0].reshape(images, rows // 2, 2 * chans)
    own = jnp.concatenate(
        own_half(jnp.stack([noise_pairs, start_pairs], axis=1), core), axis=1
    )
    own_noise, own_start = own[0], own[1]
    mine = add_parts(keep, swap_cores(send), own_start)

    mine, packed, mods = lax.optimization_barrier((mine, packed, mods))
    mine = lax.all_to_all(mine, CHIPS, 0, 0, tiled=True)

    text_pairs = text_pairs_of(
        where, packed, swap_cores(packed), mods, qk_gains, text_rows * lax.axis_size(SEQ)
    )
    received = [shift_steps(text_pairs[k], -k, steps) for k in (0, 1, 7, 2, 6, 3, 5, 4)]
    mine, received[:4], w_final = lax.optimization_barrier((mine, received[:4], w_final))
    text_pairs = jnp.concatenate(received, axis=0)
    mine, latents = sum_parts(mine, rows)
    latents = latents.reshape(-1, 2 * chans)
    theirs = swap_cores(mine)

    added = own_noise + jnp.where(place == 0, own_start, jnp.zeros_like(own_start))
    w_fin = jnp.swapaxes(w_final, 0, 1)

    x_own = own_start.astype(BF16)
    for iteration in range(ITERS):
        attended = attention(where, latents, mine, theirs, gram, qk_gains, text_pairs, chips)
        attended = lax.all_to_all(attended, CHIPS, 0, 0, tiled=True)
        contrib = output_stage(
            attended, w_out, x_own, w_latent, shifts, w_fin, step_sizes, added, steps
        )
        if iteration + 1 < ITERS:
            everyone = lax.all_to_all(contrib, "step", 0, 0, tiled=True)
            latents = scan(where, everyone, own_start, chips)
            x_own = latents[0]
            latents = lax.all_to_all(latents, CHIPS, 0, 0, tiled=True).reshape(-1, 2 * chans)
    contrib = contrib.reshape(steps * images, rows // 2, 2 * chans)
    everyone = lax.all_to_all(contrib, ("step", "core"), 0, 0, tiled=True)
    return total_rows(where, everyone, images, rows, chans)[None]


def solution(mesh):
    steps = mesh.devices.shape[0]
    fine = Mesh(mesh.devices.reshape(steps, 4, 4, 2), ("step", "y", "x", "core"))
    placed = (
        P("step", None, SEQ, None),
        P("step", None, SEQ, None),
        P("step"),
        P("step", None, None),
        P(None, SEQ, None),
        P(),
        P(SEQ, None, None, None),
        P(SEQ, None, None, None),
        P(SEQ, None, None),
        P(),
        P(),
    )
    return jax.shard_map(
        local,
        mesh=fine,
        in_specs=placed,
        out_specs=P("step", None, SEQ, None),
        check_vma=False,
    )
```
